256 devices in a mesh: section: 4 (over z_lo), ctx: 64 (over z_hi, x, y, core).
Axes of the slice: x: 4, y: 4, z: 8 (z_hi: 2, z_lo: 4; z = z_hi * 4 + z_lo), core: 2. Of those that a mesh axis runs over, the one named last changes fastest.
Arguments:
- queries: bfloat16 [512, 4096], P('section', 'ctx'), may hold values from -160 to 160
- keys: bfloat16 [32768, 4096], P(('section', 'ctx')), may hold values from -16 to 16
- values: bfloat16 [32768, 4096], P(('section', 'ctx')), may hold values from -6 to 6
- out_grad: bfloat16 [512, 4096], P('section', 'ctx'), may hold values from -12 to 12
- key_mask: int32 [32768], P(('section', 'ctx')), may hold values 0 or 1
- query_mask: int32 [512], P('section'), may hold values 0 or 1
Outputs:
- grad_queries: bfloat16 [512, 4096], P('section', 'ctx')
- grad_keys: bfloat16 [32768, 4096], P(('section', 'ctx'))
- grad_values: bfloat16 [32768, 4096], P(('section', 'ctx'))
The draws below stay inside these ranges and needn't reach their ends.
All inputs are finite; a program needn't handle non-finite values. No bound on the sum of `key_mask` or of `query_mask` on one device may be relied on, other than what follows from the above.
Results may differ from the reference program's by a relative error of at most 0.019.
Values may be sent and summed in bfloat16 or wider, within the bound.
No kernel may reach another device: no remote copies, remote signals or barrier semaphores. Data moves between devices by JAX's collectives and lax.ppermute only.
A program may use at most 128 MiB of HBM per device.

```python
import math
import jax
import jax.numpy as jnp
from jax import lax

HEADS = 64
HD = 64
LEN = 32768
LQ = 512


def draw_queries(key, part):
    key = jax.random.fold_in(key, 11)
    entries = 1.7 * jax.random.normal(key, (LQ, HEADS * HD), jnp.float32)
    return entries.astype(jnp.bfloat16)


def draw_keys(key, part):
    key = jax.random.fold_in(key, 23)
    entries = 1.7 * jax.random.normal(key, (LEN, HEADS * HD), jnp.float32)
    return entries.astype(jnp.bfloat16)


def plant(array, rng, least, high):
    longest = array.shape.index(max(array.shape))
    spots = []
    for shift in (0, 1):
        where = [jax.random.randint(jax.random.fold_in(rng, axis), (), 0, length) for axis, length in enumerate(array.shape)]
        where[longest] = (where[longest] + shift) % array.shape[longest]
        spots.append(tuple(where))
    return array.at[spots[0]].set(least).at[spots[1]].set(high)


def steps_of(stream_key, extent, split, low, high):
    def one(position, shards_of):
        draws = jax.random.uniform(jax.random.fold_in(jax.random.fold_in(stream_key, 6), position), (shards_of,), jnp.float32, low / len(split), high / len(split))
        return jnp.repeat(jnp.exp(draws), extent[position] // shards_of).reshape((-1,) + (1,) * (len(extent) - position - 1))

    loudness = one(*split[0])
    for cut in split[1:]:
        loudness = loudness * one(*cut)
    return loudness


def normal_values(own_key, dims, deviation, reach, pieces=(), kind=jnp.bfloat16):
    level = steps_of(own_key, dims, pieces, -0.22, 0.18) if pieces else 1.0
    drawn = jax.random.normal(own_key, dims, jnp.float32) * deviation * level
    return jnp.minimum(jnp.maximum(drawn, -reach), reach).astype(kind)


def setup_inputs(seed: int = 0) -> dict:
    key_list = jax.random.split(jax.random.key(seed), 7)
    return {
        "queries": draw_queries(jax.random.fold_in(key_list[6], 71), 0),
        "keys": draw_keys(jax.random.fold_in(key_list[6], 71), 0),
        "values": normal_values(key_list[2], (LEN, HEADS * HD), 1.0, 6.0, ((0, 256),)),
        "out_grad": normal_values(key_list[3], (LQ, HEADS * HD), 2.0, 12.0, ((0, 4), (1, 64))),
        "key_mask": plant((jax.random.randint(key_list[4], (LEN,), 0, 8) < 7).astype(jnp.int32), jax.random.fold_in(key_list[4], 1), 0, 1),
        "query_mask": plant((jax.random.randint(key_list[5], (LQ,), 0, 8) < 7).astype(jnp.int32), jax.random.fold_in(key_list[5], 1), 0, 1),
    }


masked_bias = -1000000000.0

def reference(queries, keys, values, out_grad, key_mask, query_mask):
    factor = 1.0 / math.sqrt(HD)
    grad_rows = out_grad * query_mask[:, None].astype(jnp.bfloat16)
    key_bias = jnp.where(key_mask == 1, 0.0, masked_bias).astype(jnp.float32)

    def per_head(head_index):
        offset = (head_index * HD).astype(jnp.int32)
        query_head = lax.dynamic_slice_in_dim(queries, offset, HD, 1)
        key_head = lax.dynamic_slice_in_dim(keys, offset, HD, 1)
        value_head = lax.dynamic_slice_in_dim(values, offset, HD, 1)
        grad_head = lax.dynamic_slice_in_dim(grad_rows, offset, HD, 1)
        logits = jnp.dot(query_head, key_head.T, preferred_element_type=jnp.float32) * factor + key_bias[None, :]
        highest = lax.optimization_barrier(jnp.max(logits, axis=1))
        summed = lax.optimization_barrier(jnp.sum(jnp.exp(logits - highest[:, None]), axis=1))
        log_total = highest + jnp.log(summed)
        weights = jnp.exp(logits - log_total[:, None])
        weights_low = weights.astype(jnp.bfloat16)
        attended = jnp.dot(weights_low, value_head, preferred_element_type=jnp.float32)
        row_inner = lax.optimization_barrier(jnp.sum(grad_head.astype(jnp.float32) * attended, axis=1))
        grad_probs = jnp.dot(grad_head, value_head.T, preferred_element_type=jnp.float32)
        grad_logits = (weights * (grad_probs - row_inner[:, None])).astype(jnp.bfloat16)
        grad_value = jnp.dot(weights_low.T, grad_head, preferred_element_type=jnp.float32)
        grad_key = jnp.dot(grad_logits.T, query_head, preferred_element_type=jnp.float32) * factor
        grad_query = jnp.dot(grad_logits, key_head, preferred_element_type=jnp.float32) * factor
        return (grad_query.astype(jnp.bfloat16), grad_key.astype(jnp.bfloat16), grad_value.astype(jnp.bfloat16))
    stacked_query, stacked_key, stacked_value = lax.map(per_head, jnp.arange(HEADS, dtype=jnp.int32))
    grad_queries = jnp.transpose(stacked_query, (1, 0, 2)).reshape(LQ, HEADS * HD)
    grad_keys = jnp.transpose(stacked_key, (1, 0, 2)).reshape(LEN, HEADS * HD)
    grad_values = jnp.transpose(stacked_value, (1, 0, 2)).reshape(LEN, HEADS * HD)
    return (grad_queries, grad_keys, grad_values)
```

```python
import functools
import math

import jax
import jax.numpy as jnp
from jax import lax
from jax.experimental import pallas as pl
from jax.experimental.pallas import tpu as pltpu
from jax.sharding import Mesh
from jax.sharding import PartitionSpec as P

HD = 64
LANES = 128
TOKENS = 512
ROWS = 128
EXTRA = 16
FACTOR = 1.0 / math.sqrt(HD)
MASKED_BIAS = -1000000000.0
AXES = ("s", "h", "x", "y", "c")
PLANE = ("x", "y", "c")
COLUMN = ("s", "h")
PEERS = 32
LAYERS = 8
f32 = jnp.float32
bf16 = jnp.bfloat16
NT = (((1,), (1,)), ((), ()))
NN = (((1,), (0,)), ((), ()))


def dot(a, b, dims=NN):
    return lax.dot_general(a, b, dims, preferred_element_type=f32)


def pack_kernel(k_ref, v_ref, m_ref, kp_ref, vp_ref):
    half = k_ref.shape[1] // 2
    for src, dst in ((k_ref, kp_ref), (v_ref, vp_ref)):
        for j in range(0, PEERS, 2):
            low = src[:, j * HD : j * HD + LANES]
            high = src[:, half + j * HD : half + j * HD + LANES]
            dst[j, :ROWS, :] = jnp.concatenate([low[:, :HD], high[:, :HD]], axis=1)
            dst[j + 1, :ROWS, :] = jnp.concatenate([low[:, HD:], high[:, HD:]], axis=1)
    mask = jnp.broadcast_to(m_ref[...].astype(f32), (EXTRA, LANES)).astype(bf16)
    for j in range(PEERS):
        kp_ref[j, ROWS:, :] = mask


def unpack_kernel(k_ref, v_ref, ko_ref, vo_ref):
    half = ko_ref.shape[1] // 2
    for src, dst in ((k_ref, ko_ref), (v_ref, vo_ref)):
        for j in range(0, PEERS, 2):
            a = src[j]
            b = src[j + 1]
            dst[:, j * HD : j * HD + LANES] = jnp.concatenate([a[:, :HD], b[:, :HD]], axis=1)
            dst[:, half + j * HD : half + j * HD + LANES] = jnp.concatenate(
                [a[:, HD:], b[:, HD:]], axis=1
            )


def spread_tokens(t_ref, q_s, d_s, qt_s, dt_s):
    lane = lax.broadcasted_iota(jnp.int32, (ROWS, LANES), 1)
    for block in range(TOKENS // ROWS):
        for head in range(2):
            both = t_ref[2 * block + head].astype(f32)
            turned = pltpu.roll(both, HD, 1)
            mine = (lane < HD) if head == 0 else (lane >= HD)
            q, d = (both, turned) if head == 0 else (turned, both)
            q = jnp.where(mine, q * FACTOR, 0.0)
            d = jnp.where(mine, d, 0.0)
            at = pl.ds(block * ROWS, ROWS)
            if q_s is not None:
                q_s[head, at, :] = q.astype(bf16)
                d_s[head, at, :] = d.astype(bf16)
            qt_s[head, :, at] = q.T.astype(bf16)
            dt_s[head, :, at] = d.T.astype(bf16)


def bias_of(k_ref, b):
    row = k_ref[b, ROWS : ROWS + EXTRA, :].astype(f32)
    square = jnp.broadcast_to(row[:1, :], (LANES, LANES)).T
    bias = jnp.where(square == 1.0, 0.0, MASKED_BIAS)
    return jnp.concatenate([bias] * (TOKENS // LANES), axis=1)


def stats_kernel(t_ref, k_ref, v_ref, o_ref, qt_s, dt_s, m_s, z_s, s_s):
    step = pl.program_id(0)

    @pl.when(step == 0)
    def _():
        spread_tokens(t_ref, None, None, qt_s, dt_s)
        m_s[...] = jnp.full(m_s.shape, -3e38, f32)
        z_s[...] = jnp.zeros(z_s.shape, f32)
        s_s[...] = jnp.zeros(s_s.shape, f32)

    for b in range(k_ref.shape[0]):
        bias = bias_of(k_ref, b)
        keys = k_ref[b, :ROWS, :]
        values = v_ref[b]
        for head in range(2):
            logits = dot(keys, qt_s[head]) + bias
            probs = dot(values, dt_s[head])
            split = (ROWS // 8, 8, TOKENS)
            logits = logits.reshape(split)
            old = m_s[head]
            new = jnp.maximum(old, jnp.max(logits, axis=0))
            scale = jnp.exp(old - new)
            weights = jnp.exp(logits - new[None])
            m_s[head] = new
            z_s[head] = z_s[head] * scale + jnp.sum(weights, axis=0)
            s_s[head] = s_s[head] * scale + jnp.sum(weights * probs.reshape(split), axis=0)

    @pl.when(step == pl.num_programs(0) - 1)
    def _():
        o_ref[...] = jnp.zeros(o_ref.shape, f32)
        for head in range(2):
            m8 = m_s[head]
            m = jnp.max(m8, axis=0, keepdims=True)
            scale = jnp.exp(m8 - m)
            z = jnp.sum(z_s[head] * scale, axis=0, keepdims=True)
            s = jnp.sum(s_s[head] * scale, axis=0, keepdims=True)
            for layer in range(LAYERS):
                o_ref[layer, head : head + 1, :] = m
                o_ref[layer, 2 + head : 3 + head, :] = z
                o_ref[layer, 4 + head : 5 + head, :] = s


def grads_kernel(
    t_ref, a_ref, k_ref, v_ref, gk_ref, gv_ref, gq_ref, q_s, d_s, qt_s, dt_s, l_s, r_s, acc_s
):
    step = pl.program_id(0)

    @pl.when(step == 0)
    def _():
        spread_tokens(t_ref, q_s, d_s, qt_s, dt_s)
        acc_s[...] = jnp.zeros(acc_s.shape, f32)
        for head in range(2):
            ms = [a_ref[i, head : head + 1, :] for i in range(LAYERS)]
            m = functools.reduce(jnp.maximum, ms)
            z = jnp.zeros_like(m)
            s = jnp.zeros_like(m)
            for i in range(LAYERS):
                scale = jnp.exp(ms[i] - m)
                z = z + scale * a_ref[i, 2 + head : 3 + head, :]
                s = s + scale * a_ref[i, 4 + head : 5 + head, :]
            l_s[head] = jnp.broadcast_to(m + jnp.log(z), (8, TOKENS))
            r_s[head] = jnp.broadcast_to(s / z, (8, TOKENS))

    for b in range(k_ref.shape[0]):
        bias = bias_of(k_ref, b)
        keys = k_ref[b, :ROWS, :]
        values = v_ref[b]
        keys_t = keys.astype(f32).T.astype(bf16)
        gk = jnp.zeros((ROWS, LANES), f32)
        gv = jnp.zeros((ROWS, LANES), f32)
        for head in range(2):
            logits = dot(keys, qt_s[head]) + bias
            probs = dot(values, dt_s[head])
            split = (ROWS // 8, 8, TOKENS)
            weights = jnp.exp(logits.reshape(split) - l_s[head][None])
            grad = weights * (probs.reshape(split) - r_s[head][None])
            weights = weights.reshape(ROWS, TOKENS).astype(bf16)
            grad = grad.reshape(ROWS, TOKENS).astype(bf16)
            gv = gv + dot(weights, d_s[head])
            gk = gk + dot(grad, q_s[head])
            acc_s[head] += dot(keys_t[head * HD : (head + 1) * HD, :], grad)
        gk_ref[b] = gk.astype(bf16)
        gv_ref[b] = gv.astype(bf16)

    @pl.when(step == pl.num_programs(0) - 1)
    def _():
        for block in range(TOKENS // ROWS):
            for head in range(2):
                part = acc_s[head, :, block * ROWS : (block + 1) * ROWS] * FACTOR
                gq_ref[2 * block + head] = part.astype(bf16)


def per_device(queries, keys, values, out_grad, key_mask, query_mask):
    vmem = pl.BlockSpec(memory_space=pltpu.VMEM)
    params = pltpu.CompilerParams(vmem_limit_bytes=48 * 1024 * 1024)
    packed_keys, packed_values = pl.pallas_call(
        pack_kernel,
        in_specs=[vmem] * 3,
        out_specs=[vmem] * 2,
        out_shape=[
            jax.ShapeDtypeStruct((PEERS, ROWS + EXTRA, LANES), bf16),
            jax.ShapeDtypeStruct((PEERS, ROWS, LANES), bf16),
        ],
        compiler_params=params,
    )(keys, values, key_mask.reshape(1, ROWS))

    grad_rows = out_grad * query_mask[:, None].astype(bf16)
    own_tokens = jnp.concatenate([queries, grad_rows], axis=1)
    copies = jnp.broadcast_to(own_tokens[None], (LAYERS,) + own_tokens.shape)
    exchange = functools.partial(lax.all_to_all, split_axis=0, concat_axis=0, tiled=True)
    tokens = exchange(copies, COLUMN)
    all_keys = exchange(packed_keys, PLANE)
    all_values = exchange(packed_values, PLANE)

    group = 4
    whole = lambda *shape: pl.BlockSpec(shape, lambda i: (0,) * len(shape))
    key_spec = pl.BlockSpec((group, ROWS + EXTRA, LANES), lambda i: (i, 0, 0))
    row_spec = pl.BlockSpec((group, ROWS, LANES), lambda i: (i, 0, 0))
    scratch = lambda *shape, dtype=bf16: pltpu.VMEM(shape, dtype)
    stats = pl.pallas_call(
        stats_kernel,
        grid=(PEERS // group,),
        in_specs=[whole(LAYERS, ROWS, LANES), key_spec, row_spec],
        out_specs=whole(LAYERS, 8, TOKENS),
        out_shape=jax.ShapeDtypeStruct((LAYERS, 8, TOKENS), f32),
        scratch_shapes=[
            scratch(2, LANES, TOKENS),
            scratch(2, LANES, TOKENS),
            scratch(2, 8, TOKENS, dtype=f32),
            scratch(2, 8, TOKENS, dtype=f32),
            scratch(2, 8, TOKENS, dtype=f32),
        ],
        compiler_params=params,
    )(tokens, all_keys, all_values)
    all_stats = exchange(stats, COLUMN)
    key_grads, value_grads, query_parts = pl.pallas_call(
        grads_kernel,
        grid=(PEERS // group,),
        in_specs=[whole(LAYERS, ROWS, LANES), whole(LAYERS, 8, TOKENS), key_spec, row_spec],
        out_specs=[row_spec, row_spec, whole(LAYERS, HD, ROWS)],
        out_shape=[
            jax.ShapeDtypeStruct((PEERS, ROWS, LANES), bf16),
            jax.ShapeDtypeStruct((PEERS, ROWS, LANES), bf16),
            jax.ShapeDtypeStruct((LAYERS, HD, ROWS), bf16),
        ],
        scratch_shapes=[
            scratch(2, TOKENS, LANES),
            scratch(2, TOKENS, LANES),
            scratch(2, LANES, TOKENS),
            scratch(2, LANES, TOKENS),
            scratch(2, 8, TOKENS, dtype=f32),
            scratch(2, 8, TOKENS, dtype=f32),
            scratch(2, HD, TOKENS, dtype=f32),
        ],
        compiler_params=params,
    )(tokens, all_stats, all_keys, all_values)
    own_values = exchange(value_grads, PLANE)
    own_keys = exchange(key_grads, PLANE)
    own_queries = exchange(query_parts, COLUMN)
    grad_queries = jnp.sum(own_queries.astype(f32), axis=0).T.astype(bf16)
    grad_keys, grad_values = pl.pallas_call(
        unpack_kernel,
        in_specs=[vmem] * 2,
        out_specs=[vmem] * 2,
        out_shape=[
            jax.ShapeDtypeStruct(keys.shape, bf16),
            jax.ShapeDtypeStruct(values.shape, bf16),
        ],
        compiler_params=params,
    )(own_keys, own_values)
    return grad_queries, grad_keys, grad_values


def solution(mesh):
    fine = Mesh(mesh.devices.reshape(4, 2, 4, 4, 2), AXES)
    ctx = ("h",) + PLANE
    rows = ("s",) + ctx
    head_spec = P("s", ctx)
    row_spec = P(rows, None)
    return jax.shard_map(
        per_device,
        mesh=fine,
        in_specs=(head_spec, row_spec, row_spec, head_spec, P(rows), P("s")),
        out_specs=(head_spec, row_spec, row_spec),
        check_vma=False,
    )
```

```python
import functools
import math

import jax
import jax.numpy as jnp
from jax import lax
from jax.experimental import pallas as pl
from jax.experimental.pallas import tpu as pltpu
from jax.sharding import Mesh
from jax.sharding import PartitionSpec as P

HD = 64
LANES = 128
TOKENS = 512
ROWS = 128
EXTRA = 16
FACTOR = 1.0 / math.sqrt(HD)
MASKED_BIAS = -1000000000.0
AXES = ("s", "h", "x", "y", "c")
PLANE = ("x", "y", "c")
COLUMN = ("h", "s")
PEERS = 32
LAYERS = 8
f32 = jnp.float32
bf16 = jnp.bfloat16
NT = (((1,), (1,)), ((), ()))
NN = (((1,), (0,)), ((), ()))


def dot(a, b, dims=NN):
    return lax.dot_general(a, b, dims, preferred_element_type=f32)


def column_of(row):
    return jnp.broadcast_to(row, (LANES, LANES)).T


def pack_kernel(k_ref, v_ref, m_ref, q_ref, d_ref, qm_ref, kv_ref, t_ref):
    half = k_ref.shape[1] // 2
    for src, base in ((k_ref, 0), (v_ref, ROWS)):
        at = pl.ds(base, ROWS)
        for j in range(0, PEERS, 2):
            low = src[:, j * HD : j * HD + LANES]
            high = src[:, half + j * HD : half + j * HD + LANES]
            kv_ref[j, at, :] = jnp.concatenate([low[:, :HD], high[:, :HD]], axis=1)
            kv_ref[j + 1, at, :] = jnp.concatenate([low[:, HD:], high[:, HD:]], axis=1)
    mask = jnp.broadcast_to(m_ref[...].astype(f32), (EXTRA, LANES)).astype(bf16)
    for j in range(PEERS):
        kv_ref[j, 2 * ROWS :, :] = mask
    rows = column_of(qm_ref[...].astype(f32))
    grad_rows = d_ref[...].astype(f32) * rows[:, :HD]
    t_ref[...] = jnp.concatenate([q_ref[...].astype(f32), grad_rows], axis=1).astype(bf16)


def unpack_kernel(g_ref, ko_ref, vo_ref):
    half = ko_ref.shape[1] // 2
    for dst, base in ((ko_ref, 0), (vo_ref, ROWS)):
        at = pl.ds(base, ROWS)
        for j in range(0, PEERS, 2):
            a = g_ref[j, at, :]
            b = g_ref[j + 1, at, :]
            dst[:, j * HD : j * HD + LANES] = jnp.concatenate([a[:, :HD], b[:, :HD]], axis=1)
            dst[:, half + j * HD : half + j * HD + LANES] = jnp.concatenate(
                [a[:, HD:], b[:, HD:]], axis=1
            )


def spread_tokens(t_ref, q_s, d_s, qt_s, dt_s):
    lane = lax.broadcasted_iota(jnp.int32, (ROWS, LANES), 1)
    for block in range(TOKENS // ROWS):
        for head in range(2):
            both = t_ref[4 * head + block].astype(f32)
            turned = pltpu.roll(both, HD, 1)
            mine = (lane < HD) if head == 0 else (lane >= HD)
            q, d = (both, turned) if head == 0 else (turned, both)
            q = jnp.where(mine, q * FACTOR, 0.0)
            d = jnp.where(mine, d, 0.0)
            at = pl.ds(block * ROWS, ROWS)
            if q_s is not None:
                q_s[head, at, :] = q.astype(bf16)
                d_s[head, at, :] = d.astype(bf16)
            qt_s[head, :, at] = q.T.astype(bf16)
            dt_s[head, :, at] = d.T.astype(bf16)


def bias_of(k_ref, b):
    row = k_ref[b, 2 * ROWS :, :].astype(f32)
    square = column_of(row[:1, :])
    bias = jnp.where(square == 1.0, 0.0, MASKED_BIAS)
    return jnp.concatenate([bias] * (TOKENS // LANES), axis=1)


def stats_kernel(t_ref, k_ref, o_ref, qt_s, dt_s, m_s, z_s, s_s):
    step = pl.program_id(0)

    @pl.when(step == 0)
    def _():
        spread_tokens(t_ref, None, None, qt_s, dt_s)
        m_s[...] = jnp.full(m_s.shape, -3e38, f32)
        z_s[...] = jnp.zeros(z_s.shape, f32)
        s_s[...] = jnp.zeros(s_s.shape, f32)

    for b in range(k_ref.shape[0]):
        bias = bias_of(k_ref, b)
        keys = k_ref[b, :ROWS, :]
        values = k_ref[b, ROWS : 2 * ROWS, :]
        for head in range(2):
            logits = dot(keys, qt_s[head]) + bias
            probs = dot(values, dt_s[head])
            split = (ROWS // 8, 8, TOKENS)
            logits = logits.reshape(split)
            old = m_s[head]
            new = jnp.maximum(old, jnp.max(logits, axis=0))
            scale = jnp.exp(old - new)
            weights = jnp.exp(logits - new[None])
            m_s[head] = new
            z_s[head] = z_s[head] * scale + jnp.sum(weights, axis=0)
            s_s[head] = s_s[head] * scale + jnp.sum(weights * probs.reshape(split), axis=0)

    @pl.when(step == pl.num_programs(0) - 1)
    def _():
        o_ref[...] = jnp.zeros(o_ref.shape, f32)
        for head in range(2):
            m8 = m_s[head]
            m = jnp.max(m8, axis=0, keepdims=True)
            scale = jnp.exp(m8 - m)
            z = jnp.sum(z_s[head] * scale, axis=0, keepdims=True)
            s = jnp.sum(s_s[head] * scale, axis=0, keepdims=True)
            for layer in range(LAYERS):
                o_ref[layer, head : head + 1, :] = m
                o_ref[layer, 2 + head : 3 + head, :] = z
                o_ref[layer, 4 + head : 5 + head, :] = s


def grads_kernel(
    t_ref, a_ref, k_ref, g_ref, gq_ref, q_s, d_s, qt_s, dt_s, l_s, r_s, acc_s
):
    step = pl.program_id(0)

    @pl.when(step == 0)
    def _():
        spread_tokens(t_ref, q_s, d_s, qt_s, dt_s)
        acc_s[...] = jnp.zeros(acc_s.shape, f32)
        for head in range(2):
            ms = [a_ref[i, head : head + 1, :] for i in range(LAYERS)]
            m = functools.reduce(jnp.maximum, ms)
            z = jnp.zeros_like(m)
            s = jnp.zeros_like(m)
            for i in range(LAYERS):
                scale = jnp.exp(ms[i] - m)
                z = z + scale * a_ref[i, 2 + head : 3 + head, :]
                s = s + scale * a_ref[i, 4 + head : 5 + head, :]
            l_s[head] = jnp.broadcast_to(m + jnp.log(z), (8, TOKENS))
            r_s[head] = jnp.broadcast_to(s / z, (8, TOKENS))

    for b in range(k_ref.shape[0]):
        bias = bias_of(k_ref, b)
        keys = k_ref[b, :ROWS, :]
        values = k_ref[b, ROWS : 2 * ROWS, :]
        keys_t = keys.astype(f32).T.astype(bf16)
        gk = jnp.zeros((ROWS, LANES), f32)
        gv = jnp.zeros((ROWS, LANES), f32)
        for head in range(2):
            logits = dot(keys, qt_s[head]) + bias
            probs = dot(values, dt_s[head])
            split = (ROWS // 8, 8, TOKENS)
            weights = jnp.exp(logits.reshape(split) - l_s[head][None])
            grad = weights * (probs.reshape(split) - r_s[head][None])
            weights = weights.reshape(ROWS, TOKENS).astype(bf16)
            grad = grad.reshape(ROWS, TOKENS).astype(bf16)
            gv = gv + dot(weights, d_s[head])
            gk = gk + dot(grad, q_s[head])
            acc_s[head] += dot(keys_t[head * HD : (head + 1) * HD, :], grad)
        g_ref[b, :ROWS, :] = gk.astype(bf16)
        g_ref[b, ROWS:, :] = gv.astype(bf16)

    @pl.when(step == pl.num_programs(0) - 1)
    def _():
        for block in range(TOKENS // ROWS):
            for head in range(2):
                part = acc_s[head, :, block * ROWS : (block + 1) * ROWS] * FACTOR
                gq_ref[4 * head + block] = part


def per_device(queries, keys, values, out_grad, key_mask, query_mask):
    vmem = pl.BlockSpec(memory_space=pltpu.VMEM)
    params = pltpu.CompilerParams(vmem_limit_bytes=48 * 1024 * 1024)
    sent_rows = 2 * ROWS + EXTRA
    packed, own_tokens = pl.pallas_call(
        pack_kernel,
        in_specs=[vmem] * 6,
        out_specs=[vmem] * 2,
        out_shape=[
            jax.ShapeDtypeStruct((PEERS, sent_rows, LANES), bf16),
            jax.ShapeDtypeStruct((ROWS, LANES), bf16),
        ],
        compiler_params=params,
    )(keys, values, key_mask.reshape(1, ROWS), queries, out_grad, query_mask.reshape(1, ROWS))
    exchange = functools.partial(lax.all_to_all, split_axis=0, concat_axis=0, tiled=True)
    tokens = lax.all_gather(own_tokens, COLUMN, axis=0, tiled=False)
    rows = exchange(packed, PLANE)

    group = 4
    whole = lambda *shape: pl.BlockSpec(shape, lambda i: (0,) * len(shape))
    in_spec = pl.BlockSpec((group, sent_rows, LANES), lambda i: (i, 0, 0))
    out_spec = pl.BlockSpec((group, 2 * ROWS, LANES), lambda i: (i, 0, 0))
    scratch = lambda *shape, dtype=bf16: pltpu.VMEM(shape, dtype)
    stats = pl.pallas_call(
        stats_kernel,
        grid=(PEERS // group,),
        in_specs=[whole(LAYERS, ROWS, LANES), in_spec],
        out_specs=whole(LAYERS, 8, TOKENS),
        out_shape=jax.ShapeDtypeStruct((LAYERS, 8, TOKENS), f32),
        scratch_shapes=[
            scratch(2, LANES, TOKENS),
            scratch(2, LANES, TOKENS),
            scratch(2, 8, TOKENS, dtype=f32),
            scratch(2, 8, TOKENS, dtype=f32),
            scratch(2, 8, TOKENS, dtype=f32),
        ],
        compiler_params=params,
    )(tokens, rows)
    all_stats = exchange(stats, COLUMN)
    grads, query_parts = pl.pallas_call(
        grads_kernel,
        grid=(PEERS // group,),
        in_specs=[whole(LAYERS, ROWS, LANES), whole(LAYERS, 8, TOKENS), in_spec],
        out_specs=[out_spec, whole(LAYERS, HD, ROWS)],
        out_shape=[
            jax.ShapeDtypeStruct((PEERS, 2 * ROWS, LANES), bf16),
            jax.ShapeDtypeStruct((LAYERS, HD, ROWS), f32),
        ],
        scratch_shapes=[
            scratch(2, TOKENS, LANES),
            scratch(2, TOKENS, LANES),
            scratch(2, LANES, TOKENS),
            scratch(2, LANES, TOKENS),
            scratch(2, 8, TOKENS, dtype=f32),
            scratch(2, 8, TOKENS, dtype=f32),
            scratch(2, HD, TOKENS, dtype=f32),
        ],
        compiler_params=params,
    )(tokens, all_stats, rows)
    own_queries = lax.psum_scatter(
        query_parts.reshape(LAYERS * HD, ROWS), COLUMN, scatter_dimension=0, tiled=True
    )
    own_rows = exchange(grads, PLANE)
    grad_queries = own_queries.T.astype(bf16)
    grad_keys, grad_values = pl.pallas_call(
        unpack_kernel,
        in_specs=[vmem],
        out_specs=[vmem] * 2,
        out_shape=[
            jax.ShapeDtypeStruct(keys.shape, bf16),
            jax.ShapeDtypeStruct(values.shape, bf16),
        ],
        compiler_params=params,
    )(own_rows)
    return grad_queries, grad_keys, grad_values


def solution(mesh):
    fine = Mesh(mesh.devices.reshape(4, 2, 4, 4, 2), AXES)
    ctx = ("h",) + PLANE
    rows = ("s",) + ctx
    head_spec = P("s", ctx)
    row_spec = P(rows, None)
    return jax.shard_map(
        per_device,
        mesh=fine,
        in_specs=(head_spec, row_spec, row_spec, head_spec, P(rows), P("s")),
        out_specs=(head_spec, row_spec, row_spec),
        check_vma=False,
    )
```

```python
import functools
import math

import jax
import jax.numpy as jnp
from jax import lax
from jax.experimental import pallas as pl
from jax.experimental.pallas import tpu as pltpu
from jax.sharding import Mesh
from jax.sharding import PartitionSpec as P

HD = 64
LANES = 128
TOKENS = 512
ROWS = 128
EXTRA = 16
STATS_JOINED = 4
GRADS_JOINED = 8
MIB = 1024 * 1024
FACTOR = 1.0 / math.sqrt(HD)
MASKED_BIAS = -1000000000.0
AXES = ("s", "h", "x", "y", "c")
PLANE = ("x", "y", "c")
COLUMN = ("h", "s")
PEERS = 32
LAYERS = 8
f32 = jnp.float32
bf16 = jnp.bfloat16
NT = (((1,), (1,)), ((), ()))
NN = (((1,), (0,)), ((), ()))


def dot(a, b, dims=NN):
    return lax.dot_general(a, b, dims, preferred_element_type=f32)


def column_of(row):
    return jnp.broadcast_to(row, (LANES, LANES)).T


def pack_kernel(k_ref, v_ref, m_ref, q_ref, d_ref, qm_ref, kv_ref, t_ref, *scratch):
    k_s, v_s, m_s, q_s, d_s, qm_s, kv_s, t_s, in_sems, small_sems, out_sems = scratch
    steps = in_sems.shape[0]
    half = k_ref.shape[1] // 2
    width = half // steps
    copy = pltpu.make_async_copy
    small = ((m_ref, m_s), (q_ref, q_s), (d_ref, d_s), (qm_ref, qm_s))
    small = [copy(src, dst, small_sems.at[i]) for i, (src, dst) in enumerate(small)]
    loads = []
    for step in range(steps):
        for i, (src, dst) in enumerate(((k_ref, k_s), (v_ref, v_s))):
            for side in range(2):
                at = pl.ds(side * half + step * width, width)
                sem = in_sems.at[step, 2 * i + side]
                loads.append(copy(src.at[:, at], dst.at[:, at], sem))
    for load in small + loads:
        load.start()
    for load in small:
        load.wait()
    t_s[:HD, :] = (q_s[...].astype(f32) * FACTOR).astype(bf16)
    t_s[HD:, :] = (d_s[...].astype(f32) * qm_s[...].astype(f32)).astype(bf16)
    stores = [copy(t_s, t_ref, out_sems.at[steps])]
    stores[0].start()
    mask = jnp.broadcast_to(m_s[...].astype(f32), (EXTRA, LANES)).astype(bf16)
    for step in range(steps):
        for load in loads[4 * step : 4 * step + 4]:
            load.wait()
        first = step * width // HD
        for j in range(first, first + width // HD, 2):
            for src, base in ((k_s, 0), (v_s, ROWS)):
                at = pl.ds(base, ROWS)
                low = src[:, j * HD : j * HD + LANES]
                high = src[:, half + j * HD : half + j * HD + LANES]
                kv_s[j, at, :] = jnp.concatenate([low[:, :HD], high[:, :HD]], axis=1)
                kv_s[j + 1, at, :] = jnp.concatenate([low[:, HD:], high[:, HD:]], axis=1)
            kv_s[j, 2 * ROWS :, :] = mask
            kv_s[j + 1, 2 * ROWS :, :] = mask
        at = pl.ds(first, width // HD)
        store = copy(kv_s.at[at], kv_ref.at[at], out_sems.at[step])
        store.start()
        stores.append(store)
    for store in stores:
        store.wait()


def unpack_kernel(g_ref, ko_ref, vo_ref, k_s, v_s, sems):
    steps = sems.shape[0]
    half = ko_ref.shape[1] // 2
    width = half // steps
    stores = []
    for step in range(steps):
        first = step * width // HD
        for i, (dst, out, base) in enumerate(((k_s, ko_ref, 0), (v_s, vo_ref, ROWS))):
            at = pl.ds(base, ROWS)
            for j in range(first, first + width // HD, 2):
                a = g_ref[j, at, :]
                b = g_ref[j + 1, at, :]
                low = jnp.concatenate([a[:, :HD], b[:, :HD]], axis=1)
                high = jnp.concatenate([a[:, HD:], b[:, HD:]], axis=1)
                dst[:, j * HD : j * HD + LANES] = low
                dst[:, half + j * HD : half + j * HD + LANES] = high
            for side in range(2):
                at = pl.ds(side * half + step * width, width)
                sem = sems.at[step, 2 * i + side]
                store = pltpu.make_async_copy(dst.at[:, at], out.at[:, at], sem)
                store.start()
                stores.append(store)
    for store in stores:
        store.wait()


def layer_index():
    return lax.axis_index("h") * 4 + lax.axis_index("s")


def spread_tokens(t_refs, t_s, q_s, d_s, qt_s, dt_s):
    layer = layer_index()
    for r in range(LAYERS):
        t_s[lax.rem(layer + LAYERS - r, LAYERS)] = t_refs[r][...]
    qt_s[...] = jnp.zeros(qt_s.shape, bf16)
    dt_s[...] = jnp.zeros(dt_s.shape, bf16)
    for block in range(TOKENS // ROWS):
        at = pl.ds(block * ROWS, ROWS)
        for head in range(2):
            mine = pl.ds(head * HD, HD)
            qt_s[head, mine, at] = t_s[4 * head + block, :HD, :]
            dt_s[head, mine, at] = t_s[4 * head + block, HD:, :]
            if q_s is not None:
                q_s[head, at, :] = qt_s[head, :, at].astype(f32).T.astype(bf16)
                d_s[head, at, :] = dt_s[head, :, at].astype(f32).T.astype(bf16)


def bias_of(k_ref, first, count):
    parts = []
    for b in range(first, first + count):
        row = k_ref[b, 2 * ROWS :, :].astype(f32)
        square = column_of(row[:1, :])
        bias = jnp.where(square == 1.0, 0.0, MASKED_BIAS)
        parts.append(jnp.concatenate([bias] * (TOKENS // LANES), axis=1))
    return jnp.concatenate(parts, axis=0)


def block_of(k_ref, first, count, base):
    return k_ref[first : first + count, base : base + ROWS, :].reshape(count * ROWS, LANES)


def stats_kernel(*refs):
    t_refs, (k_ref, o_ref, t_s, qt_s, dt_s, m_s, z_s, s_s) = refs[:LAYERS], refs[LAYERS:]
    step = pl.program_id(0)

    @pl.when(step == 0)
    def _():
        spread_tokens(t_refs, t_s, None, None, qt_s, dt_s)
        m_s[...] = jnp.full(m_s.shape, -3e38, f32)
        z_s[...] = jnp.zeros(z_s.shape, f32)
        s_s[...] = jnp.zeros(s_s.shape, f32)

    count = STATS_JOINED
    split = (count * ROWS // 8, 8, TOKENS)
    for b in range(0, k_ref.shape[0], count):
        bias = bias_of(k_ref, b, count)
        keys = block_of(k_ref, b, count, 0)
        values = block_of(k_ref, b, count, ROWS)
        for head in range(2):
            logits = dot(keys, qt_s[head]) + bias
            probs = dot(values, dt_s[head])
            logits = logits.reshape(split)
            old = m_s[head]
            new = jnp.maximum(old, jnp.max(logits, axis=0))
            scale = jnp.exp(old - new)
            weights = jnp.exp(logits - new[None])
            m_s[head] = new
            z_s[head] = z_s[head] * scale + jnp.sum(weights, axis=0)
            s_s[head] = s_s[head] * scale + jnp.sum(weights * probs.reshape(split), axis=0)

    @pl.when(step == pl.num_programs(0) - 1)
    def _():
        o_ref[...] = jnp.zeros(o_ref.shape, f32)
        for head in range(2):
            m8 = m_s[head]
            m = jnp.max(m8, axis=0, keepdims=True)
            scale = jnp.exp(m8 - m)
            z = jnp.sum(z_s[head] * scale, axis=0, keepdims=True)
            s = jnp.sum(s_s[head] * scale, axis=0, keepdims=True)
            for layer in range(LAYERS):
                o_ref[layer, head : head + 1, :] = m
                o_ref[layer, 2 + head : 3 + head, :] = z
                o_ref[layer, 4 + head : 5 + head, :] = s


def grads_kernel(*refs):
    t_refs, (a_ref, k_ref, g_ref), refs = refs[:LAYERS], refs[LAYERS : LAYERS + 3], refs[LAYERS + 3 :]
    gq_refs, (t_s, q_s, d_s, qt_s, dt_s, l_s, r_s, acc_s, part_s) = refs[:LAYERS], refs[LAYERS:]
    step = pl.program_id(0)

    @pl.when(step == 0)
    def _():
        spread_tokens(t_refs, t_s, q_s, d_s, qt_s, dt_s)
        acc_s[...] = jnp.zeros(acc_s.shape, f32)
        for head in range(2):
            ms = [a_ref[i, head : head + 1, :] for i in range(LAYERS)]
            m = functools.reduce(jnp.maximum, ms)
            z = jnp.zeros_like(m)
            s = jnp.zeros_like(m)
            for i in range(LAYERS):
                scale = jnp.exp(ms[i] - m)
                z = z + scale * a_ref[i, 2 + head : 3 + head, :]
                s = s + scale * a_ref[i, 4 + head : 5 + head, :]
            l_s[head] = jnp.broadcast_to(m + jnp.log(z), (8, TOKENS))
            r_s[head] = jnp.broadcast_to(s / z, (8, TOKENS))

    count = GRADS_JOINED
    split = (count * ROWS // 8, 8, TOKENS)
    for b in range(0, k_ref.shape[0], count):
        bias = bias_of(k_ref, b, count)
        keys = block_of(k_ref, b, count, 0)
        values = block_of(k_ref, b, count, ROWS)
        keys_t = keys.astype(f32).T.astype(bf16)
        gk = jnp.zeros(keys.shape, f32)
        gv = jnp.zeros(keys.shape, f32)
        for head in range(2):
            logits = dot(keys, qt_s[head]) + bias
            probs = dot(values, dt_s[head])
            weights = jnp.exp(logits.reshape(split) - l_s[head][None])
            grad = weights * (probs.reshape(split) - r_s[head][None])
            weights = weights.reshape(count * ROWS, TOKENS).astype(bf16)
            grad = grad.reshape(count * ROWS, TOKENS).astype(bf16)
            gv = gv + dot(weights, d_s[head])
            gk = gk + dot(grad, q_s[head])
            acc_s[head] += dot(keys_t[head * HD : (head + 1) * HD, :], grad)
        shape = (count, ROWS, LANES)
        g_ref[b : b + count, :ROWS, :] = gk.astype(bf16).reshape(shape)
        g_ref[b : b + count, ROWS:, :] = gv.astype(bf16).reshape(shape)

    @pl.when(step == pl.num_programs(0) - 1)
    def _():
        for block in range(TOKENS // ROWS):
            for head in range(2):
                part = acc_s[head, :, block * ROWS : (block + 1) * ROWS] * FACTOR
                part_s[4 * head + block] = part.astype(bf16)
        for r in range(LAYERS):
            gq_refs[r][...] = part_s[lax.rem(layer_index() + r, LAYERS)]


def permuted(array, distance):
    place = lambda z: (z % 4) * 2 + z // 4
    pairs = [(place(z), place((z + distance) % LAYERS)) for z in range(LAYERS)]
    return lax.ppermute(array, ("s", "h"), pairs)


def permuted_parts(arrays):
    return [arrays[0]] + [permuted(arrays[r], r) for r in range(1, LAYERS)]


def per_device(queries, keys, values, out_grad, key_mask, query_mask):
    vmem = pl.BlockSpec(memory_space=pltpu.VMEM)
    hbm = pl.BlockSpec(memory_space=pl.ANY)
    limit = lambda mib: pltpu.CompilerParams(vmem_limit_bytes=mib * MIB)
    whole = lambda *shape: pl.BlockSpec(shape, lambda i: (0,) * len(shape))
    scratch = lambda *shape, dtype=bf16: pltpu.VMEM(shape, dtype)
    dma = pltpu.SemaphoreType.DMA
    i32 = jnp.int32
    sent_rows = 2 * ROWS + EXTRA
    steps = 8
    packed, own_tokens = pl.pallas_call(
        pack_kernel,
        in_specs=[hbm] * 6,
        out_specs=[hbm] * 2,
        out_shape=[
            pltpu.HBM((PEERS, sent_rows, LANES), bf16),
            pltpu.HBM((2 * HD, ROWS), bf16),
        ],
        scratch_shapes=[
            scratch(*keys.shape),
            scratch(*values.shape),
            scratch(1, ROWS, dtype=i32),
            scratch(HD, ROWS),
            scratch(HD, ROWS),
            scratch(1, ROWS, dtype=i32),
            scratch(PEERS, sent_rows, LANES),
            scratch(2 * HD, ROWS),
            dma((steps, 4)),
            dma((4,)),
            dma((steps + 1,)),
        ],
        compiler_params=limit(60),
    )(
        keys,
        values,
        key_mask.reshape(1, ROWS),
        queries.T,
        out_grad.T,
        query_mask.reshape(1, ROWS),
    )
    exchange = functools.partial(lax.all_to_all, split_axis=0, concat_axis=0, tiled=True)
    rows = exchange(packed, PLANE)
    tokens = permuted_parts([own_tokens] * LAYERS)

    group = 8
    in_spec = pl.BlockSpec((group, sent_rows, LANES), lambda i: (i, 0, 0))
    out_spec = pl.BlockSpec((group, 2 * ROWS, LANES), lambda i: (i, 0, 0))
    token_specs = [whole(2 * HD, ROWS)] * LAYERS
    stats = pl.pallas_call(
        stats_kernel,
        grid=(PEERS // group,),
        in_specs=token_specs + [in_spec],
        out_specs=whole(LAYERS, 8, TOKENS),
        out_shape=pltpu.HBM((LAYERS, 8, TOKENS), f32),
        scratch_shapes=[
            scratch(LAYERS, 2 * HD, ROWS),
            scratch(2, LANES, TOKENS),
            scratch(2, LANES, TOKENS),
            scratch(2, 8, TOKENS, dtype=f32),
            scratch(2, 8, TOKENS, dtype=f32),
            scratch(2, 8, TOKENS, dtype=f32),
        ],
        compiler_params=limit(40),
    )(*tokens, rows)
    all_stats = exchange(stats, COLUMN)
    grads, *query_parts = pl.pallas_call(
        grads_kernel,
        grid=(PEERS // group,),
        in_specs=token_specs + [whole(LAYERS, 8, TOKENS), in_spec],
        out_specs=[out_spec] + [whole(HD, ROWS)] * LAYERS,
        out_shape=[pltpu.HBM((PEERS, 2 * ROWS, LANES), bf16)]
        + [pltpu.HBM((HD, ROWS), bf16)] * LAYERS,
        scratch_shapes=[
            scratch(LAYERS, 2 * HD, ROWS),
            scratch(2, TOKENS, LANES),
            scratch(2, TOKENS, LANES),
            scratch(2, LANES, TOKENS),
            scratch(2, LANES, TOKENS),
            scratch(2, 8, TOKENS, dtype=f32),
            scratch(2, 8, TOKENS, dtype=f32),
            scratch(2, HD, TOKENS, dtype=f32),
            scratch(LAYERS, HD, ROWS),
        ],
        compiler_params=limit(40),
    )(*tokens, all_stats, rows)
    own_rows = exchange(grads, PLANE)
    own_parts = permuted_parts(query_parts)
    total = functools.reduce(jnp.add, [part.astype(f32) for part in own_parts])
    grad_queries = total.astype(bf16).T
    grad_keys, grad_values = pl.pallas_call(
        unpack_kernel,
        in_specs=[vmem],
        out_specs=[hbm] * 2,
        out_shape=[pltpu.HBM(keys.shape, bf16), pltpu.HBM(values.shape, bf16)],
        scratch_shapes=[scratch(*keys.shape), scratch(*values.shape), dma((steps, 4))],
        compiler_params=limit(16),
    )(own_rows)
    return grad_queries, grad_keys, grad_values


def solution(mesh):
    fine = Mesh(mesh.devices.reshape(4, 2, 4, 4, 2), AXES)
    ctx = ("h",) + PLANE
    rows = ("s",) + ctx
    head_spec = P("s", ctx)
    row_spec = P(rows, None)
    return jax.shard_map(
        per_device,
        mesh=fine,
        in_specs=(head_spec, row_spec, row_spec, head_spec, P(rows), P("s")),
        out_specs=(head_spec, row_spec, row_spec),
        check_vma=False,
    )
```

```python
import functools
import math

import jax
import jax.numpy as jnp
from jax import lax
from jax.experimental import pallas as pl
from jax.experimental.pallas import tpu as pltpu
from jax.sharding import Mesh
from jax.sharding import PartitionSpec as P

HD = 64
LANES = 128
TOKENS = 512
ROWS = 128
EXTRA = 16
JOINED = 4
MIB = 1024 * 1024
FACTOR = 1.0 / math.sqrt(HD)
MASKED_BIAS = -1000000000.0
AXES = ("s", "h", "x", "y", "c")
PLANE = ("x", "y", "c")
COLUMN = ("h", "s")
PEERS = 32
LAYERS = 8
f32 = jnp.float32
bf16 = jnp.bfloat16
NT = (((1,), (1,)), ((), ()))
NN = (((1,), (0,)), ((), ()))


def dot(a, b, dims=NN):
    return lax.dot_general(a, b, dims, preferred_element_type=f32)


def column_of(row):
    return jnp.broadcast_to(row, (LANES, LANES)).T


def pack_kernel(k_ref, v_ref, m_ref, q_ref, d_ref, qm_ref, kv_ref, t_ref, *scratch):
    k_s, v_s, m_s, q_s, d_s, qm_s, kv_s, t_s, in_sems, small_sems, out_sems = scratch
    steps = in_sems.shape[0]
    half = k_ref.shape[1] // 2
    width = half // steps
    copy = pltpu.make_async_copy
    small = ((m_ref, m_s), (q_ref, q_s), (d_ref, d_s), (qm_ref, qm_s))
    small = [copy(src, dst, small_sems.at[i]) for i, (src, dst) in enumerate(small)]
    loads = []
    for step in range(steps):
        for i, (src, dst) in enumerate(((k_ref, k_s), (v_ref, v_s))):
            for side in range(2):
                at = pl.ds(side * half + step * width, width)
                sem = in_sems.at[step, 2 * i + side]
                loads.append(copy(src.at[:, at], dst.at[:, at], sem))
    for load in small + loads:
        load.start()
    for load in small:
        load.wait()
    t_s[:HD, :] = (q_s[...].astype(f32) * FACTOR).astype(bf16)
    t_s[HD:, :] = (d_s[...].astype(f32) * qm_s[...].astype(f32)).astype(bf16)
    stores = [copy(t_s, t_ref, out_sems.at[steps])]
    stores[0].start()
    mask = jnp.broadcast_to(m_s[...].astype(f32), (EXTRA, LANES)).astype(bf16)
    for step in range(steps):
        for load in loads[4 * step : 4 * step + 4]:
            load.wait()
        first = step * width // HD
        for j in range(first, first + width // HD, 2):
            for src, base in ((k_s, 0), (v_s, ROWS)):
                at = pl.ds(base, ROWS)
                low = src[:, j * HD : j * HD + LANES]
                high = src[:, half + j * HD : half + j * HD + LANES]
                kv_s[j, at, :] = jnp.concatenate([low[:, :HD], high[:, :HD]], axis=1)
                kv_s[j + 1, at, :] = jnp.concatenate([low[:, HD:], high[:, HD:]], axis=1)
            kv_s[j, 2 * ROWS :, :] = mask
            kv_s[j + 1, 2 * ROWS :, :] = mask
        at = pl.ds(first, width // HD)
        store = copy(kv_s.at[at], kv_ref.at[at], out_sems.at[step])
        store.start()
        stores.append(store)
    for store in stores:
        store.wait()


def unpack_kernel(g_ref, ko_ref, vo_ref, k_s, v_s, sems):
    steps = sems.shape[0]
    half = ko_ref.shape[1] // 2
    width = half // steps
    stores = []
    for step in range(steps):
        first = step * width // HD
        for i, (dst, out, base) in enumerate(((k_s, ko_ref, 0), (v_s, vo_ref, ROWS))):
            at = pl.ds(base, ROWS)
            for j in range(first, first + width // HD, 2):
                a = g_ref[j, at, :]
                b = g_ref[j + 1, at, :]
                low = jnp.concatenate([a[:, :HD], b[:, :HD]], axis=1)
                high = jnp.concatenate([a[:, HD:], b[:, HD:]], axis=1)
                dst[:, j * HD : j * HD + LANES] = low
                dst[:, half + j * HD : half + j * HD + LANES] = high
            for side in range(2):
                at = pl.ds(side * half + step * width, width)
                sem = sems.at[step, 2 * i + side]
                store = pltpu.make_async_copy(dst.at[:, at], out.at[:, at], sem)
                store.start()
                stores.append(store)
    for store in stores:
        store.wait()


def layer_index():
    return lax.axis_index("h") * 4 + lax.axis_index("s")


def spread_kernel(*refs):
    t_refs, (q_ref, d_ref, qt_ref, dt_ref, t_s) = refs[:LAYERS], refs[LAYERS:]
    layer = layer_index()
    for r in range(LAYERS):
        t_s[lax.rem(layer + LAYERS - r, LAYERS)] = t_refs[r][...]
    qt_ref[...] = jnp.zeros(qt_ref.shape, bf16)
    dt_ref[...] = jnp.zeros(dt_ref.shape, bf16)
    for block in range(TOKENS // ROWS):
        at = pl.ds(block * ROWS, ROWS)
        for head in range(2):
            mine = pl.ds(head * HD, HD)
            qt_ref[head, mine, at] = t_s[4 * head + block, :HD, :]
            dt_ref[head, mine, at] = t_s[4 * head + block, HD:, :]
            q_ref[head, at, :] = qt_ref[head, :, at].astype(f32).T.astype(bf16)
            d_ref[head, at, :] = dt_ref[head, :, at].astype(f32).T.astype(bf16)


def bias_of(k_ref, first):
    parts = []
    for i in range(JOINED):
        row = k_ref[first + i, 2 * ROWS :, :].astype(f32)
        square = column_of(row[:1, :])
        bias = jnp.where(square == 1.0, 0.0, MASKED_BIAS)
        parts.append(jnp.concatenate([bias] * (TOKENS // LANES), axis=1))
    return jnp.concatenate(parts, axis=0)


def block_of(k_ref, first, count, base):
    return k_ref[pl.ds(first, count), base : base + ROWS, :].reshape(count * ROWS, LANES)


SPLIT = (JOINED * ROWS // 8, 8, TOKENS)
FLAT = (JOINED * ROWS, TOKENS)


def stats_kernel(k_ref, qt_ref, dt_ref, o_ref, p_ref, b_ref, m_s, z_s, s_s):
    m_s[...] = jnp.full(m_s.shape, -3e38, f32)
    z_s[...] = jnp.zeros(z_s.shape, f32)
    s_s[...] = jnp.zeros(s_s.shape, f32)

    def one_pair(pair, carry):
        for b in (2 * pair, 2 * pair + 1):
            first = b * JOINED
            bias = bias_of(k_ref, first)
            keys = block_of(k_ref, first, JOINED, 0)
            values = block_of(k_ref, first, JOINED, ROWS)
            for head in range(2):
                logits = (dot(keys, qt_ref[head]) + bias).reshape(SPLIT)
                probs = dot(values, dt_ref[head]).reshape(SPLIT)
                old = m_s[head]
                new = jnp.maximum(old, jnp.max(logits, axis=0))
                scale = jnp.exp(old - new)
                weights = jnp.exp(logits - new[None])
                m_s[head] = new
                b_ref[head, b] = new
                z_s[head] = z_s[head] * scale + jnp.sum(weights, axis=0)
                s_s[head] = s_s[head] * scale + jnp.sum(weights * probs, axis=0)
                p_ref[head, b] = weights.reshape(FLAT).astype(bf16)
        return carry

    lax.fori_loop(0, PEERS // JOINED // 2, one_pair, 0)
    o_ref[...] = jnp.zeros(o_ref.shape, f32)
    for head in range(2):
        m = jnp.max(m_s[head], axis=0, keepdims=True)
        scale = jnp.exp(m_s[head] - m)
        z = jnp.sum(z_s[head] * scale, axis=0, keepdims=True)
        s = jnp.sum(s_s[head] * scale, axis=0, keepdims=True)
        for layer in range(LAYERS):
            o_ref[layer, head : head + 1, :] = m
            o_ref[layer, 2 + head : 3 + head, :] = z
            o_ref[layer, 4 + head : 5 + head, :] = s


def grads_kernel(*refs):
    a_ref, k_ref, q_ref, d_ref, dt_ref, p_ref, b_ref, g_ref = refs[:8]
    gq_refs, (l_s, r_s, acc_s, part_s, g_s, sems) = refs[8 : 8 + LAYERS], refs[8 + LAYERS :]
    acc_s[...] = jnp.zeros(acc_s.shape, f32)
    for head in range(2):
        ms = [a_ref[i, head : head + 1, :] for i in range(LAYERS)]
        m = functools.reduce(jnp.maximum, ms)
        z = jnp.zeros_like(m)
        s = jnp.zeros_like(m)
        for i in range(LAYERS):
            scale = jnp.exp(ms[i] - m)
            z = z + scale * a_ref[i, 2 + head : 3 + head, :]
            s = s + scale * a_ref[i, 4 + head : 5 + head, :]
        l_s[head] = jnp.broadcast_to(m + jnp.log(z), (8, TOKENS))
        r_s[head] = jnp.broadcast_to(s / z, (8, TOKENS))

    count = 2 * JOINED
    flat = (count * ROWS, TOKENS)

    def store_of(pair):
        at = pl.ds(pair * count, count)
        return pltpu.make_async_copy(g_s.at[at], g_ref.at[at], sems.at[pair])

    def one_pair(pair, carry):
        first = pair * count
        keys_t = block_of(k_ref, first, count, 0).astype(f32).T.astype(bf16)
        values = block_of(k_ref, first, count, ROWS)
        gk = jnp.zeros(values.shape, f32)
        gv = jnp.zeros(values.shape, f32)
        for head in range(2):
            blocks = pl.ds(2 * pair, 2)
            scale = jnp.exp(b_ref[head, blocks] - l_s[head][None])
            probs = dot(values, dt_ref[head]).reshape((2,) + SPLIT)
            weights = p_ref[head, blocks].astype(f32).reshape((2,) + SPLIT) * scale[:, None]
            grad = weights * (probs - r_s[head])
            weights = weights.reshape(flat).astype(bf16)
            grad = grad.reshape(flat).astype(bf16)
            gv = gv + dot(weights, d_ref[head])
            gk = gk + dot(grad, q_ref[head])
            acc_s[head] += dot(keys_t[head * HD : (head + 1) * HD, :], grad)
        shape = (count, ROWS, LANES)
        g_s[pl.ds(first, count), :ROWS, :] = gk.astype(bf16).reshape(shape)
        g_s[pl.ds(first, count), ROWS:, :] = gv.astype(bf16).reshape(shape)
        store_of(pair).start()
        return carry

    pairs = PEERS // count
    lax.fori_loop(0, pairs, one_pair, 0)
    for block in range(TOKENS // ROWS):
        for head in range(2):
            part = acc_s[head, :, block * ROWS : (block + 1) * ROWS] * FACTOR
            part_s[4 * head + block] = part.astype(bf16)
    for r in range(LAYERS):
        gq_refs[r][...] = part_s[lax.rem(layer_index() + r, LAYERS)]
    for pair in range(pairs):
        store_of(pair).wait()


def permuted(array, distance):
    place = lambda z: (z % 4) * 2 + z // 4
    pairs = [(place(z), place((z + distance) % LAYERS)) for z in range(LAYERS)]
    return lax.ppermute(array, ("s", "h"), pairs)


def permuted_parts(arrays):
    return [arrays[0]] + [permuted(arrays[r], r) for r in range(1, LAYERS)]


def per_device(queries, keys, values, out_grad, key_mask, query_mask):
    vmem = pl.BlockSpec(memory_space=pltpu.VMEM)
    hbm = pl.BlockSpec(memory_space=pl.ANY)
    limit = lambda mib: pltpu.CompilerParams(vmem_limit_bytes=mib * MIB)
    whole = lambda *shape: pl.BlockSpec(shape, lambda i: (0,) * len(shape))
    scratch = lambda *shape, dtype=bf16: pltpu.VMEM(shape, dtype)
    dma = pltpu.SemaphoreType.DMA
    i32 = jnp.int32
    sent_rows = 2 * ROWS + EXTRA
    steps = 2
    packed, own_tokens = pl.pallas_call(
        pack_kernel,
        in_specs=[hbm] * 6,
        out_specs=[hbm] * 2,
        out_shape=[
            pltpu.HBM((PEERS, sent_rows, LANES), bf16),
            pltpu.HBM((2 * HD, ROWS), bf16),
        ],
        scratch_shapes=[
            scratch(*keys.shape),
            scratch(*values.shape),
            scratch(1, ROWS, dtype=i32),
            scratch(HD, ROWS),
            scratch(HD, ROWS),
            scratch(1, ROWS, dtype=i32),
            scratch(PEERS, sent_rows, LANES),
            scratch(2 * HD, ROWS),
            dma((steps, 4)),
            dma((4,)),
            dma((steps + 1,)),
        ],
        compiler_params=limit(60),
    )(
        keys,
        values,
        key_mask.reshape(1, ROWS),
        queries.T,
        out_grad.T,
        query_mask.reshape(1, ROWS),
    )
    exchange = functools.partial(lax.all_to_all, split_axis=0, concat_axis=0, tiled=True)
    rows = exchange(packed, PLANE)
    tokens = permuted_parts([own_tokens] * LAYERS)

    blocks = PEERS // JOINED
    shape = jax.ShapeDtypeStruct
    q, d, qt, dt = pl.pallas_call(
        spread_kernel,
        in_specs=[vmem] * LAYERS,
        out_specs=[vmem] * 4,
        out_shape=[shape((2, TOKENS, LANES), bf16)] * 2 + [shape((2, LANES, TOKENS), bf16)] * 2,
        scratch_shapes=[scratch(LAYERS, 2 * HD, ROWS)],
        compiler_params=limit(8),
    )(*tokens)
    stats, weights, maxima = pl.pallas_call(
        stats_kernel,
        in_specs=[vmem] * 3,
        out_specs=[vmem] * 3,
        out_shape=[
            shape((LAYERS, 8, TOKENS), f32),
            shape((2, blocks) + FLAT, bf16),
            shape((2, blocks, 8, TOKENS), f32),
        ],
        scratch_shapes=[
            scratch(2, 8, TOKENS, dtype=f32),
            scratch(2, 8, TOKENS, dtype=f32),
            scratch(2, 8, TOKENS, dtype=f32),
        ],
        compiler_params=limit(24),
    )(rows, qt, dt)
    all_stats = exchange(stats, COLUMN)
    grads, *query_parts = pl.pallas_call(
        grads_kernel,
        in_specs=[vmem] * 7,
        out_specs=[hbm] + [vmem] * LAYERS,
        out_shape=[pltpu.HBM((PEERS, 2 * ROWS, LANES), bf16)] + [shape((HD, ROWS), bf16)] * LAYERS,
        scratch_shapes=[
            scratch(2, 8, TOKENS, dtype=f32),
            scratch(2, 8, TOKENS, dtype=f32),
            scratch(2, HD, TOKENS, dtype=f32),
            scratch(LAYERS, HD, ROWS),
            scratch(PEERS, 2 * ROWS, LANES),
            dma((blocks // 2,)),
        ],
        compiler_params=limit(32),
    )(all_stats, rows, q, d, dt, weights, maxima)
    own_rows = exchange(grads, PLANE)
    own_parts = permuted_parts(query_parts)
    total = functools.reduce(jnp.add, [part.astype(f32) for part in own_parts])
    grad_queries = total.astype(bf16).T
    grad_keys, grad_values = pl.pallas_call(
        unpack_kernel,
        in_specs=[vmem],
        out_specs=[hbm] * 2,
        out_shape=[pltpu.HBM(keys.shape, bf16), pltpu.HBM(values.shape, bf16)],
        scratch_shapes=[scratch(*keys.shape), scratch(*values.shape), dma((steps, 4))],
        compiler_params=limit(16),
    )(own_rows)
    return grad_queries, grad_keys, grad_values


def solution(mesh):
    fine = Mesh(mesh.devices.reshape(4, 2, 4, 4, 2), AXES)
    ctx = ("h",) + PLANE
    rows = ("s",) + ctx
    head_spec = P("s", ctx)
    row_spec = P(rows, None)
    return jax.shard_map(
        per_device,
        mesh=fine,
        in_specs=(head_spec, row_spec, row_spec, head_spec, P(rows), P("s")),
        out_specs=(head_spec, row_spec, row_spec),
        check_vma=False,
    )
```

```python
import functools
import math

import jax
import jax.numpy as jnp
from jax import lax
from jax.experimental import pallas as pl
from jax.experimental.pallas import tpu as pltpu
from jax.sharding import Mesh
from jax.sharding import PartitionSpec as P

HD = 64
LANES = 128
TOKENS = 512
ROWS = 128
EXTRA = 16
JOINED = 2
UNROLLED = 8
MERGED = 4
MIB = 1024 * 1024
FACTOR = 1.0 / math.sqrt(HD)
MASKED_BIAS = -1000000000.0
AXES = ("s", "h", "x", "y", "c")
PLANE = ("x", "y", "c")
COLUMN = ("h", "s")
PEERS = 32
LAYERS = 8
f32 = jnp.float32
bf16 = jnp.bfloat16
NT = (((1,), (1,)), ((), ()))
NN = (((1,), (0,)), ((), ()))


def dot(a, b, dims=NN):
    return lax.dot_general(a, b, dims, preferred_element_type=f32)


def column_of(row):
    return jnp.broadcast_to(row, (LANES, LANES)).T


def pack_kernel(k_ref, v_ref, m_ref, q_ref, d_ref, qm_ref, kv_ref, t_ref, *scratch):
    k_s, v_s, m_s, q_s, d_s, qm_s, kv_s, t_s, in_sems, small_sems, out_sems = scratch
    steps = in_sems.shape[0]
    half = k_ref.shape[1] // 2
    width = half // steps
    copy = pltpu.make_async_copy
    small = ((m_ref, m_s), (q_ref, q_s), (d_ref, d_s), (qm_ref, qm_s))
    small = [copy(src, dst, small_sems.at[i]) for i, (src, dst) in enumerate(small)]
    loads = []
    for step in range(steps):
        for i, (src, dst) in enumerate(((k_ref, k_s), (v_ref, v_s))):
            for side in range(2):
                at = pl.ds(side * half + step * width, width)
                sem = in_sems.at[step, 2 * i + side]
                loads.append(copy(src.at[:, at], dst.at[:, at], sem))
    for load in small + loads:
        load.start()
    for load in small:
        load.wait()
    t_s[:HD, :] = (q_s[...].astype(f32) * FACTOR).astype(bf16)
    t_s[HD:, :] = (d_s[...].astype(f32) * qm_s[...].astype(f32)).astype(bf16)
    stores = [copy(t_s, t_ref, out_sems.at[steps])]
    stores[0].start()
    mask = jnp.broadcast_to(m_s[...].astype(f32), (EXTRA, LANES)).astype(bf16)
    for step in range(steps):
        for load in loads[4 * step : 4 * step + 4]:
            load.wait()
        first = step * width // HD
        for j in range(first, first + width // HD, 2):
            for src, base in ((k_s, 0), (v_s, ROWS)):
                at = pl.ds(base, ROWS)
                low = src[:, j * HD : j * HD + LANES]
                high = src[:, half + j * HD : half + j * HD + LANES]
                kv_s[j, at, :] = jnp.concatenate([low[:, :HD], high[:, :HD]], axis=1)
                kv_s[j + 1, at, :] = jnp.concatenate([low[:, HD:], high[:, HD:]], axis=1)
            kv_s[j, 2 * ROWS :, :] = mask
            kv_s[j + 1, 2 * ROWS :, :] = mask
        at = pl.ds(first, width // HD)
        store = copy(kv_s.at[at], kv_ref.at[at], out_sems.at[step])
        store.start()
        stores.append(store)
    for store in stores:
        store.wait()


def unpack_kernel(g_ref, ko_ref, vo_ref, k_s, v_s, sems):
    steps = sems.shape[0]
    half = ko_ref.shape[1] // 2
    width = half // steps
    stores = []
    for step in range(steps):
        first = step * width // HD
        for i, (dst, out, base) in enumerate(((k_s, ko_ref, 0), (v_s, vo_ref, ROWS))):
            at = pl.ds(base, ROWS)
            for j in range(first, first + width // HD, 2):
                a = g_ref[j, at, :]
                b = g_ref[j + 1, at, :]
                low = jnp.concatenate([a[:, :HD], b[:, :HD]], axis=1)
                high = jnp.concatenate([a[:, HD:], b[:, HD:]], axis=1)
                dst[:, j * HD : j * HD + LANES] = low
                dst[:, half + j * HD : half + j * HD + LANES] = high
            for side in range(2):
                at = pl.ds(side * half + step * width, width)
                sem = sems.at[step, 2 * i + side]
                store = pltpu.make_async_copy(dst.at[:, at], out.at[:, at], sem)
                store.start()
                stores.append(store)
    for store in stores:
        store.wait()


def layer_index():
    return lax.axis_index("h") * 4 + lax.axis_index("s")


def spread_kernel(*refs):
    t_refs, (q_ref, d_ref, qt_ref, dt_ref, t_s) = refs[:LAYERS], refs[LAYERS:]
    layer = layer_index()
    for r in range(LAYERS):
        t_s[lax.rem(layer + LAYERS - r, LAYERS)] = t_refs[r][...]
    qt_ref[...] = jnp.zeros(qt_ref.shape, bf16)
    dt_ref[...] = jnp.zeros(dt_ref.shape, bf16)
    for block in range(TOKENS // ROWS):
        at = pl.ds(block * ROWS, ROWS)
        for head in range(2):
            mine = pl.ds(head * HD, HD)
            qt_ref[head, mine, at] = t_s[4 * head + block, :HD, :]
            dt_ref[head, mine, at] = t_s[4 * head + block, HD:, :]
            q_ref[head, at, :] = qt_ref[head, :, at].astype(f32).T.astype(bf16)
            d_ref[head, at, :] = dt_ref[head, :, at].astype(f32).T.astype(bf16)


def bias_of(k_ref, first):
    parts = []
    for i in range(JOINED):
        row = k_ref[first + i, 2 * ROWS :, :].astype(f32)
        square = column_of(row[:1, :])
        bias = jnp.where(square == 1.0, 0.0, MASKED_BIAS)
        parts.append(jnp.concatenate([bias] * (TOKENS // LANES), axis=1))
    return jnp.concatenate(parts, axis=0)


def block_of(k_ref, first, count, base):
    return k_ref[pl.ds(first, count), base : base + ROWS, :].reshape(count * ROWS, LANES)


SPLIT = (JOINED * ROWS // 8, 8, TOKENS)
FLAT = (JOINED * ROWS, TOKENS)


def stats_kernel(k_ref, qt_ref, dt_ref, o_ref, p_ref, b_ref, m_s, z_s, s_s):
    m_s[...] = jnp.full(m_s.shape, -3e38, f32)
    z_s[...] = jnp.zeros(z_s.shape, f32)
    s_s[...] = jnp.zeros(s_s.shape, f32)

    def one_step(step, carry):
        for part in range(UNROLLED):
            b = step * UNROLLED + part
            first = b * JOINED
            bias = bias_of(k_ref, first)
            keys = block_of(k_ref, first, JOINED, 0)
            values = block_of(k_ref, first, JOINED, ROWS)
            for head in range(2):
                logits = (dot(keys, qt_ref[head]) + bias).reshape(SPLIT)
                probs = dot(values, dt_ref[head]).reshape(SPLIT)
                old = m_s[head]
                new = jnp.maximum(old, jnp.max(logits, axis=0))
                scale = jnp.exp(old - new)
                weights = jnp.exp(logits - new[None])
                m_s[head] = new
                b_ref[head, b] = new
                z_s[head] = z_s[head] * scale + jnp.sum(weights, axis=0)
                s_s[head] = s_s[head] * scale + jnp.sum(weights * probs, axis=0)
                p_ref[head, b] = weights.reshape(FLAT).astype(bf16)
        return carry

    lax.fori_loop(0, PEERS // JOINED // UNROLLED, one_step, 0)
    for head in range(2):
        m = jnp.max(m_s[head], axis=0, keepdims=True)
        scale = jnp.exp(m_s[head] - m)
        z = jnp.sum(z_s[head] * scale, axis=0, keepdims=True)
        s = jnp.sum(s_s[head] * scale, axis=0, keepdims=True)
        for i, row in enumerate((m + jnp.log(z), s / z)):
            for half in range(2):
                at = 4 * i + 2 * head + half
                part = row[:, half * (TOKENS // 2) : (half + 1) * (TOKENS // 2)]
                for layer in range(LAYERS):
                    o_ref[layer, at : at + 1, :] = part


def grads_kernel(*refs):
    a_ref, k_ref, q_ref, d_ref, dt_ref, p_ref, b_ref, g_ref = refs[:8]
    gq_refs, (l_s, r_s, acc_s, part_s, g_s, sems) = refs[8 : 8 + LAYERS], refs[8 + LAYERS :]
    acc_s[...] = jnp.zeros(acc_s.shape, f32)
    for head in range(2):
        for half in range(2):
            at = 2 * head + half
            sums = [a_ref[i, at : at + 1, :] for i in range(LAYERS)]
            inner = [a_ref[i, 4 + at : 5 + at, :] for i in range(LAYERS)]
            m = functools.reduce(jnp.maximum, sums)
            shares = [jnp.exp(part - m) for part in sums]
            z = functools.reduce(jnp.add, shares)
            s = functools.reduce(jnp.add, [x * y for x, y in zip(shares, inner)])
            lanes = pl.ds(half * (TOKENS // 2), TOKENS // 2)
            l_s[head, :, lanes] = jnp.broadcast_to(m + jnp.log(z), (8, TOKENS // 2))
            r_s[head, :, lanes] = jnp.broadcast_to(s / z, (8, TOKENS // 2))

    count = MERGED * JOINED
    flat = (count * ROWS, TOKENS)
    parts = (MERGED,) + SPLIT

    def store_of(step):
        at = pl.ds(step * count, count)
        return pltpu.make_async_copy(g_s.at[at], g_ref.at[at], sems.at[step])

    def one_step(step, carry):
        first = step * count
        keys_t = block_of(k_ref, first, count, 0).astype(f32).T.astype(bf16)
        values = block_of(k_ref, first, count, ROWS)
        gk = jnp.zeros(values.shape, f32)
        gv = jnp.zeros(values.shape, f32)
        for head in range(2):
            blocks = pl.ds(MERGED * step, MERGED)
            scale = jnp.exp(b_ref[head, blocks] - l_s[head][None])
            probs = dot(values, dt_ref[head]).reshape(parts)
            weights = p_ref[head, blocks].astype(f32).reshape(parts) * scale[:, None]
            grad = weights * (probs - r_s[head])
            weights = weights.reshape(flat).astype(bf16)
            grad = grad.reshape(flat).astype(bf16)
            gv = gv + dot(weights, d_ref[head])
            gk = gk + dot(grad, q_ref[head])
            acc_s[head] += dot(keys_t[head * HD : (head + 1) * HD, :], grad)
        shape = (count, ROWS, LANES)
        g_s[pl.ds(first, count), :ROWS, :] = gk.astype(bf16).reshape(shape)
        g_s[pl.ds(first, count), ROWS:, :] = gv.astype(bf16).reshape(shape)
        store_of(step).start()
        return carry

    steps = PEERS // count
    lax.fori_loop(0, steps, one_step, 0)
    for block in range(TOKENS // ROWS):
        for head in range(2):
            part = acc_s[head, :, block * ROWS : (block + 1) * ROWS] * FACTOR
            part_s[4 * head + block] = part.astype(bf16)
    for r in range(LAYERS):
        gq_refs[r][...] = part_s[lax.rem(layer_index() + r, LAYERS)]
    for step in range(steps):
        store_of(step).wait()


def permuted(array, distance):
    place = lambda z: (z % 4) * 2 + z // 4
    pairs = [(place(z), place((z + distance) % LAYERS)) for z in range(LAYERS)]
    return lax.ppermute(array, ("s", "h"), pairs)


def permuted_parts(arrays):
    return [arrays[0]] + [permuted(arrays[r], r) for r in range(1, LAYERS)]


def per_device(queries, keys, values, out_grad, key_mask, query_mask):
    vmem = pl.BlockSpec(memory_space=pltpu.VMEM)
    hbm = pl.BlockSpec(memory_space=pl.ANY)
    limit = lambda mib: pltpu.CompilerParams(vmem_limit_bytes=mib * MIB)
    whole = lambda *shape: pl.BlockSpec(shape, lambda i: (0,) * len(shape))
    scratch = lambda *shape, dtype=bf16: pltpu.VMEM(shape, dtype)
    dma = pltpu.SemaphoreType.DMA
    i32 = jnp.int32
    sent_rows = 2 * ROWS + EXTRA
    steps = 2
    packed, own_tokens = pl.pallas_call(
        pack_kernel,
        in_specs=[hbm] * 6,
        out_specs=[hbm] * 2,
        out_shape=[
            pltpu.HBM((PEERS, sent_rows, LANES), bf16),
            pltpu.HBM((2 * HD, ROWS), bf16),
        ],
        scratch_shapes=[
            scratch(*keys.shape),
            scratch(*values.shape),
            scratch(1, ROWS, dtype=i32),
            scratch(HD, ROWS),
            scratch(HD, ROWS),
            scratch(1, ROWS, dtype=i32),
            scratch(PEERS, sent_rows, LANES),
            scratch(2 * HD, ROWS),
            dma((steps, 4)),
            dma((4,)),
            dma((steps + 1,)),
        ],
        compiler_params=limit(60),
    )(
        keys,
        values,
        key_mask.reshape(1, ROWS),
        queries.T,
        out_grad.T,
        query_mask.reshape(1, ROWS),
    )
    exchange = functools.partial(lax.all_to_all, split_axis=0, concat_axis=0, tiled=True)
    rows = exchange(packed, PLANE)
    tokens = permuted_parts([own_tokens] * LAYERS)

    blocks = PEERS // JOINED
    shape = jax.ShapeDtypeStruct
    q, d, qt, dt = pl.pallas_call(
        spread_kernel,
        in_specs=[vmem] * LAYERS,
        out_specs=[vmem] * 4,
        out_shape=[shape((2, TOKENS, LANES), bf16)] * 2 + [shape((2, LANES, TOKENS), bf16)] * 2,
        scratch_shapes=[scratch(LAYERS, 2 * HD, ROWS)],
        compiler_params=limit(8),
    )(*tokens)
    stats, weights, maxima = pl.pallas_call(
        stats_kernel,
        in_specs=[vmem] * 3,
        out_specs=[vmem] * 3,
        out_shape=[
            shape((LAYERS, 8, TOKENS // 2), f32),
            shape((2, blocks) + FLAT, bf16),
            shape((2, blocks, 8, TOKENS), f32),
        ],
        scratch_shapes=[
            scratch(2, 8, TOKENS, dtype=f32),
            scratch(2, 8, TOKENS, dtype=f32),
            scratch(2, 8, TOKENS, dtype=f32),
        ],
        compiler_params=limit(24),
    )(rows, qt, dt)
    all_stats = exchange(stats, COLUMN)
    grads, *query_parts = pl.pallas_call(
        grads_kernel,
        in_specs=[vmem] * 7,
        out_specs=[hbm] + [vmem] * LAYERS,
        out_shape=[pltpu.HBM((PEERS, 2 * ROWS, LANES), bf16)] + [shape((HD, ROWS), bf16)] * LAYERS,
        scratch_shapes=[
            scratch(2, 8, TOKENS, dtype=f32),
            scratch(2, 8, TOKENS, dtype=f32),
            scratch(2, HD, TOKENS, dtype=f32),
            scratch(LAYERS, HD, ROWS),
            scratch(PEERS, 2 * ROWS, LANES),
            dma((blocks // MERGED,)),
        ],
        compiler_params=limit(32),
    )(all_stats, rows, q, d, dt, weights, maxima)
    own_rows = exchange(grads, PLANE)
    own_parts = permuted_parts(query_parts)
    total = functools.reduce(jnp.add, [part.astype(f32) for part in own_parts])
    grad_queries = total.astype(bf16).T
    grad_keys, grad_values = pl.pallas_call(
        unpack_kernel,
        in_specs=[vmem],
        out_specs=[hbm] * 2,
        out_shape=[pltpu.HBM(keys.shape, bf16), pltpu.HBM(values.shape, bf16)],
        scratch_shapes=[scratch(*keys.shape), scratch(*values.shape), dma((steps, 4))],
        compiler_params=limit(16),
    )(own_rows)
    return grad_queries, grad_keys, grad_values


def solution(mesh):
    fine = Mesh(mesh.devices.reshape(4, 2, 4, 4, 2), AXES)
    ctx = ("h",) + PLANE
    rows = ("s",) + ctx
    head_spec = P("s", ctx)
    row_spec = P(rows, None)
    return jax.shard_map(
        per_device,
        mesh=fine,
        in_specs=(head_spec, row_spec, row_spec, head_spec, P(rows), P("s")),
        out_specs=(head_spec, row_spec, row_spec),
        check_vma=False,
    )
```

```python
import functools
import math

import jax
import jax.numpy as jnp
from jax import lax
from jax.experimental import pallas as pl
from jax.experimental.pallas import tpu as pltpu
from jax.sharding import Mesh
from jax.sharding import PartitionSpec as P

HD = 64
LANES = 128
TOKENS = 512
ROWS = 128
EXTRA = 16
JOINED = 2
UNROLLED = 8
MERGED = 4
MIB = 1024 * 1024
FACTOR = 1.0 / math.sqrt(HD)
MASKED_BIAS = -1000000000.0
AXES = ("s", "h", "x", "y", "c")
PLANE = ("x", "y", "c")
COLUMN = ("h", "s")
PEERS = 32
LAYERS = 8
f32 = jnp.float32
bf16 = jnp.bfloat16
NT = (((1,), (1,)), ((), ()))
NN = (((1,), (0,)), ((), ()))


def dot(a, b, dims=NN):
    return lax.dot_general(a, b, dims, preferred_element_type=f32)


def column_of(row):
    return jnp.broadcast_to(row, (LANES, LANES)).T


def pack_kernel(k_ref, v_ref, m_ref, q_ref, d_ref, qm_ref, kv_ref, t_ref, *scratch):
    k_s, v_s, m_s, q_s, d_s, qm_s, kv_s, t_s, in_sems, small_sems, out_sems = scratch
    steps = in_sems.shape[0]
    half = k_ref.shape[1] // 2
    width = half // steps
    copy = pltpu.make_async_copy
    small = ((m_ref, m_s), (q_ref, q_s), (d_ref, d_s), (qm_ref, qm_s))
    small = [copy(src, dst, small_sems.at[i]) for i, (src, dst) in enumerate(small)]
    loads = []
    for step in range(steps):
        for i, (src, dst) in enumerate(((k_ref, k_s), (v_ref, v_s))):
            for side in range(2):
                at = pl.ds(side * half + step * width, width)
                sem = in_sems.at[step, 2 * i + side]
                loads.append(copy(src.at[:, at], dst.at[:, at], sem))
    for load in small + loads:
        load.start()
    for load in small:
        load.wait()
    t_s[:HD, :] = (q_s[...].astype(f32) * FACTOR).astype(bf16)
    t_s[HD:, :] = (d_s[...].astype(f32) * qm_s[...].astype(f32)).astype(bf16)
    stores = [copy(t_s, t_ref, out_sems.at[steps])]
    stores[0].start()
    mask = jnp.broadcast_to(m_s[...].astype(f32), (EXTRA, LANES)).astype(bf16)
    for step in range(steps):
        for load in loads[4 * step : 4 * step + 4]:
            load.wait()
        first = step * width // HD
        for j in range(first, first + width // HD, 2):
            for src, base in ((k_s, 0), (v_s, ROWS)):
                at = pl.ds(base, ROWS)
                low = src[:, j * HD : j * HD + LANES]
                high = src[:, half + j * HD : half + j * HD + LANES]
                kv_s[j, at, :] = jnp.concatenate([low[:, :HD], high[:, :HD]], axis=1)
                kv_s[j + 1, at, :] = jnp.concatenate([low[:, HD:], high[:, HD:]], axis=1)
            kv_s[j, 2 * ROWS :, :] = mask
            kv_s[j + 1, 2 * ROWS :, :] = mask
        at = pl.ds(first, width // HD)
        store = copy(kv_s.at[at], kv_ref.at[at], out_sems.at[step])
        store.start()
        stores.append(store)
    for store in stores:
        store.wait()


def unpack_kernel(g_ref, ko_ref, vo_ref, k_s, v_s, sems):
    steps = sems.shape[0]
    half = ko_ref.shape[1] // 2
    width = half // steps
    stores = []
    for step in range(steps):
        first = step * width // HD
        for i, (dst, out, base) in enumerate(((k_s, ko_ref, 0), (v_s, vo_ref, ROWS))):
            at = pl.ds(base, ROWS)
            for j in range(first, first + width // HD, 2):
                a = g_ref[j, at, :]
                b = g_ref[j + 1, at, :]
                low = jnp.concatenate([a[:, :HD], b[:, :HD]], axis=1)
                high = jnp.concatenate([a[:, HD:], b[:, HD:]], axis=1)
                dst[:, j * HD : j * HD + LANES] = low
                dst[:, half + j * HD : half + j * HD + LANES] = high
            for side in range(2):
                at = pl.ds(side * half + step * width, width)
                sem = sems.at[step, 2 * i + side]
                store = pltpu.make_async_copy(dst.at[:, at], out.at[:, at], sem)
                store.start()
                stores.append(store)
    for store in stores:
        store.wait()


def layer_index():
    return lax.axis_index("h") * 4 + lax.axis_index("s")


def spread_kernel(*refs):
    t_refs, (q_ref, d_ref, qt_ref, dt_ref, t_s) = refs[:LAYERS], refs[LAYERS:]
    layer = layer_index()
    for r in range(LAYERS):
        t_s[lax.rem(layer + LAYERS - r, LAYERS)] = t_refs[r][...]
    qt_ref[...] = jnp.zeros(qt_ref.shape, bf16)
    dt_ref[...] = jnp.zeros(dt_ref.shape, bf16)
    for block in range(TOKENS // ROWS):
        at = pl.ds(block * ROWS, ROWS)
        for head in range(2):
            mine = pl.ds(head * HD, HD)
            qt_ref[head, mine, at] = t_s[4 * head + block, :HD, :]
            dt_ref[head, mine, at] = t_s[4 * head + block, HD:, :]
            q_ref[head, at, :] = qt_ref[head, :, at].astype(f32).T.astype(bf16)
            d_ref[head, at, :] = dt_ref[head, :, at].astype(f32).T.astype(bf16)


def bias_of(k_ref, first):
    parts = []
    for i in range(JOINED):
        row = k_ref[first + i, 2 * ROWS :, :].astype(f32)
        square = column_of(row[:1, :])
        bias = jnp.where(square == 1.0, 0.0, MASKED_BIAS)
        parts.append(jnp.concatenate([bias] * (TOKENS // LANES), axis=1))
    return jnp.concatenate(parts, axis=0)


def block_of(k_ref, first, count, base):
    return k_ref[pl.ds(first, count), base : base + ROWS, :].reshape(count * ROWS, LANES)


SPLIT = (JOINED * ROWS // 8, 8, TOKENS)
FLAT = (JOINED * ROWS, TOKENS)


def stats_kernel(k_ref, qt_ref, dt_ref, o_ref, p_ref, b_ref, m_s, z_s, s_s):
    m_s[...] = jnp.full(m_s.shape, -3e38, f32)
    z_s[...] = jnp.zeros(z_s.shape, f32)
    s_s[...] = jnp.zeros(s_s.shape, f32)

    def one_step(step, carry):
        for part in range(UNROLLED):
            b = step * UNROLLED + part
            first = b * JOINED
            bias = bias_of(k_ref, first)
            keys = block_of(k_ref, first, JOINED, 0)
            values = block_of(k_ref, first, JOINED, ROWS)
            for head in range(2):
                logits = (dot(keys, qt_ref[head]) + bias).reshape(SPLIT)
                probs = dot(values, dt_ref[head]).reshape(SPLIT)
                old = m_s[head]
                new = jnp.maximum(old, jnp.max(logits, axis=0))
                scale = jnp.exp(old - new)
                weights = jnp.exp(logits - new[None])
                m_s[head] = new
                b_ref[head, b] = new
                z_s[head] = z_s[head] * scale + jnp.sum(weights, axis=0)
                s_s[head] = s_s[head] * scale + jnp.sum(weights * probs, axis=0)
                p_ref[head, b] = weights.reshape(FLAT).astype(bf16)
        return carry

    lax.fori_loop(0, PEERS // JOINED // UNROLLED, one_step, 0)
    for head in range(2):
        m = jnp.max(m_s[head], axis=0, keepdims=True)
        scale = jnp.exp(m_s[head] - m)
        z = jnp.sum(z_s[head] * scale, axis=0, keepdims=True)
        s = jnp.sum(s_s[head] * scale, axis=0, keepdims=True)
        for i, row in enumerate((m + jnp.log(z), s / z)):
            for half in range(2):
                at = 4 * i + 2 * head + half
                part = row[:, half * (TOKENS // 2) : (half + 1) * (TOKENS // 2)]
                for layer in range(LAYERS):
                    o_ref[layer, at : at + 1, :] = part


def grads_kernel(*refs):
    a_ref, k_ref, q_ref, d_ref, dt_ref, p_ref, b_ref, g_ref, gl_ref, kt_ref = refs[:10]
    l_s, r_s, gl_s, kt_s, g_s, sems = refs[10:]
    for head in range(2):
        for half in range(2):
            at = 2 * head + half
            sums = [a_ref[i, at : at + 1, :] for i in range(LAYERS)]
            inner = [a_ref[i, 4 + at : 5 + at, :] for i in range(LAYERS)]
            m = functools.reduce(jnp.maximum, sums)
            shares = [jnp.exp(part - m) for part in sums]
            z = functools.reduce(jnp.add, shares)
            s = functools.reduce(jnp.add, [x * y for x, y in zip(shares, inner)])
            lanes = pl.ds(half * (TOKENS // 2), TOKENS // 2)
            l_s[head, :, lanes] = jnp.broadcast_to(m + jnp.log(z), (8, TOKENS // 2))
            r_s[head, :, lanes] = jnp.broadcast_to(s / z, (8, TOKENS // 2))

    count = MERGED * JOINED
    flat = (count * ROWS, TOKENS)
    parts = (MERGED,) + SPLIT

    def stores_of(step):
        at = pl.ds(step * count, count)
        pairs = [(gl_s.at[head, step], gl_ref.at[head, step]) for head in range(2)]
        pairs += [(kt_s.at[step], kt_ref.at[step]), (g_s.at[at], g_ref.at[at])]
        copy = pltpu.make_async_copy
        return [copy(src, dst, sems.at[step, i]) for i, (src, dst) in enumerate(pairs)]

    def one_step(step, carry):
        first = step * count
        stores = stores_of(step)
        kt_s[step] = block_of(k_ref, first, count, 0).astype(f32).T.astype(bf16)
        stores[2].start()
        values = block_of(k_ref, first, count, ROWS)
        both_weights, both_grads = [], []
        for head in range(2):
            blocks = pl.ds(MERGED * step, MERGED)
            scale = jnp.exp(b_ref[head, blocks] - l_s[head][None])
            probs = dot(values, dt_ref[head]).reshape(parts)
            weights = p_ref[head, blocks].astype(f32).reshape(parts) * scale[:, None]
            grad = weights * (probs - r_s[head])
            weights = weights.reshape(flat).astype(bf16)
            grad = grad.reshape(flat).astype(bf16)
            gl_s[head, step] = grad
            stores[head].start()
            both_weights.append(weights)
            both_grads.append(grad)
        gv = dot(jnp.concatenate(both_weights, axis=1), d_ref[...].reshape(2 * TOKENS, LANES))
        gk = dot(jnp.concatenate(both_grads, axis=1), q_ref[...].reshape(2 * TOKENS, LANES))
        shape = (count, ROWS, LANES)
        g_s[pl.ds(first, count), :ROWS, :] = gk.astype(bf16).reshape(shape)
        g_s[pl.ds(first, count), ROWS:, :] = gv.astype(bf16).reshape(shape)
        stores[3].start()
        return carry

    steps = PEERS // count
    lax.fori_loop(0, steps, one_step, 0)
    for step in range(steps):
        for store in stores_of(step):
            store.wait()


def query_kernel(gl_ref, kt_ref, *refs):
    gq_refs, (gl_s, kt_s, part_s, sems) = refs[:LAYERS], refs[LAYERS:]
    steps = sems.shape[0]
    copy = pltpu.make_async_copy
    loads = []
    for step in range(steps):
        pairs = [(gl_ref.at[head, step], gl_s.at[head, step]) for head in range(2)]
        pairs += [(kt_ref.at[step], kt_s.at[step])]
        loads.append([copy(src, dst, sems.at[step, i]) for i, (src, dst) in enumerate(pairs)])
    for load in sum(loads, []):
        load.start()
    sums = [0.0, 0.0]
    for step in range(steps):
        for load in loads[step]:
            load.wait()
        for head in range(2):
            mine = kt_s[step, head * HD : (head + 1) * HD, :]
            sums[head] = sums[head] + dot(mine, gl_s[head, step])
    for block in range(TOKENS // ROWS):
        for head in range(2):
            part = sums[head][:, block * ROWS : (block + 1) * ROWS] * FACTOR
            part_s[4 * head + block] = part.astype(bf16)
    for r in range(LAYERS):
        gq_refs[r][...] = part_s[lax.rem(layer_index() + r, LAYERS)]


def permuted(array, distance):
    place = lambda z: (z % 4) * 2 + z // 4
    pairs = [(place(z), place((z + distance) % LAYERS)) for z in range(LAYERS)]
    return lax.ppermute(array, ("s", "h"), pairs)


def permuted_parts(arrays):
    return [arrays[0]] + [permuted(arrays[r], r) for r in range(1, LAYERS)]


def per_device(queries, keys, values, out_grad, key_mask, query_mask):
    vmem = pl.BlockSpec(memory_space=pltpu.VMEM)
    hbm = pl.BlockSpec(memory_space=pl.ANY)
    limit = lambda mib: pltpu.CompilerParams(vmem_limit_bytes=mib * MIB)
    whole = lambda *shape: pl.BlockSpec(shape, lambda i: (0,) * len(shape))
    scratch = lambda *shape, dtype=bf16: pltpu.VMEM(shape, dtype)
    dma = pltpu.SemaphoreType.DMA
    i32 = jnp.int32
    sent_rows = 2 * ROWS + EXTRA
    steps = 2
    packed, own_tokens = pl.pallas_call(
        pack_kernel,
        in_specs=[hbm] * 6,
        out_specs=[hbm] * 2,
        out_shape=[
            pltpu.HBM((PEERS, sent_rows, LANES), bf16),
            pltpu.HBM((2 * HD, ROWS), bf16),
        ],
        scratch_shapes=[
            scratch(*keys.shape),
            scratch(*values.shape),
            scratch(1, ROWS, dtype=i32),
            scratch(HD, ROWS),
            scratch(HD, ROWS),
            scratch(1, ROWS, dtype=i32),
            scratch(PEERS, sent_rows, LANES),
            scratch(2 * HD, ROWS),
            dma((steps, 4)),
            dma((4,)),
            dma((steps + 1,)),
        ],
        compiler_params=limit(60),
    )(
        keys,
        values,
        key_mask.reshape(1, ROWS),
        queries.T,
        out_grad.T,
        query_mask.reshape(1, ROWS),
    )
    exchange = functools.partial(lax.all_to_all, split_axis=0, concat_axis=0, tiled=True)
    rows = exchange(packed, PLANE)
    tokens = permuted_parts([own_tokens] * LAYERS)

    blocks = PEERS // JOINED
    shape = jax.ShapeDtypeStruct
    q, d, qt, dt = pl.pallas_call(
        spread_kernel,
        in_specs=[vmem] * LAYERS,
        out_specs=[vmem] * 4,
        out_shape=[shape((2, TOKENS, LANES), bf16)] * 2 + [shape((2, LANES, TOKENS), bf16)] * 2,
        scratch_shapes=[scratch(LAYERS, 2 * HD, ROWS)],
        compiler_params=limit(8),
    )(*tokens)
    stats, weights, maxima = pl.pallas_call(
        stats_kernel,
        in_specs=[vmem] * 3,
        out_specs=[vmem] * 3,
        out_shape=[
            shape((LAYERS, 8, TOKENS // 2), f32),
            shape((2, blocks) + FLAT, bf16),
            shape((2, blocks, 8, TOKENS), f32),
        ],
        scratch_shapes=[
            scratch(2, 8, TOKENS, dtype=f32),
            scratch(2, 8, TOKENS, dtype=f32),
            scratch(2, 8, TOKENS, dtype=f32),
        ],
        compiler_params=limit(24),
    )(rows, qt, dt)
    all_stats = exchange(stats, COLUMN)
    steps = blocks // MERGED
    merged = MERGED * JOINED * ROWS
    grads, grad_logits, keys_t = pl.pallas_call(
        grads_kernel,
        in_specs=[vmem] * 7,
        out_specs=[hbm] * 3,
        out_shape=[
            pltpu.HBM((PEERS, 2 * ROWS, LANES), bf16),
            pltpu.HBM((2, steps, merged, TOKENS), bf16),
            pltpu.HBM((steps, LANES, merged), bf16),
        ],
        scratch_shapes=[
            scratch(2, 8, TOKENS, dtype=f32),
            scratch(2, 8, TOKENS, dtype=f32),
            scratch(2, steps, merged, TOKENS),
            scratch(steps, LANES, merged),
            scratch(PEERS, 2 * ROWS, LANES),
            dma((steps, 4)),
        ],
        compiler_params=limit(38),
    )(all_stats, rows, q, d, dt, weights, maxima)
    own_rows = exchange(grads, PLANE)
    query_parts = pl.pallas_call(
        query_kernel,
        in_specs=[hbm] * 2,
        out_specs=[vmem] * LAYERS,
        out_shape=[shape((HD, ROWS), bf16)] * LAYERS,
        scratch_shapes=[
            scratch(2, steps, merged, TOKENS),
            scratch(steps, LANES, merged),
            scratch(LAYERS, HD, ROWS),
            dma((steps, 3)),
        ],
        compiler_params=limit(48),
        cost_estimate=pl.CostEstimate(
            flops=4 * PEERS * ROWS * HD * TOKENS, bytes_accessed=9 * MIB, transcendentals=0
        ),
    )(grad_logits, keys_t)
    own_parts = permuted_parts(query_parts)
    total = functools.reduce(jnp.add, [part.astype(f32) for part in own_parts])
    grad_queries = total.astype(bf16).T
    grad_keys, grad_values = pl.pallas_call(
        unpack_kernel,
        in_specs=[vmem],
        out_specs=[hbm] * 2,
        out_shape=[pltpu.HBM(keys.shape, bf16), pltpu.HBM(values.shape, bf16)],
        scratch_shapes=[scratch(*keys.shape), scratch(*values.shape), dma((steps, 4))],
        compiler_params=limit(16),
    )(own_rows)
    return grad_queries, grad_keys, grad_values


def solution(mesh):
    fine = Mesh(mesh.devices.reshape(4, 2, 4, 4, 2), AXES)
    ctx = ("h",) + PLANE
    rows = ("s",) + ctx
    head_spec = P("s", ctx)
    row_spec = P(rows, None)
    return jax.shard_map(
        per_device,
        mesh=fine,
        in_specs=(head_spec, row_spec, row_spec, head_spec, P(rows), P("s")),
        out_specs=(head_spec, row_spec, row_spec),
        check_vma=False,
    )
```

```python
import functools
import math

import jax
import jax.numpy as jnp
from jax import lax
from jax.experimental import pallas as pl
from jax.experimental.pallas import tpu as pltpu
from jax.sharding import Mesh
from jax.sharding import PartitionSpec as P

HD = 64
LANES = 128
TOKENS = 512
ROWS = 128
EXTRA = 16
JOINED = 2
UNROLLED = 16
MERGED = 4
MIB = 1024 * 1024
FACTOR = 1.0 / math.sqrt(HD)
MASKED_BIAS = -1000000000.0
AXES = ("s", "h", "x", "y", "c")
PLANE = ("x", "y", "c")
COLUMN = ("h", "s")
PEERS = 32
LAYERS = 8
f32 = jnp.float32
bf16 = jnp.bfloat16
NT = (((1,), (1,)), ((), ()))
NN = (((1,), (0,)), ((), ()))


def dot(a, b, dims=NN):
    return lax.dot_general(a, b, dims, preferred_element_type=f32)


def column_of(row):
    return jnp.broadcast_to(row, (LANES, LANES)).T


def pack_kernel(k_ref, v_ref, m_ref, q_ref, d_ref, qm_ref, kv_ref, t_ref, *scratch):
    k_s, v_s, m_s, q_s, d_s, qm_s, kv_s, t_s, in_sems, small_sems, out_sems = scratch
    steps = in_sems.shape[0]
    half = k_ref.shape[1] // 2
    width = half // steps
    copy = pltpu.make_async_copy
    small = ((m_ref, m_s), (q_ref, q_s), (d_ref, d_s), (qm_ref, qm_s))
    small = [copy(src, dst, small_sems.at[i]) for i, (src, dst) in enumerate(small)]
    loads = []
    for step in range(steps):
        for i, (src, dst) in enumerate(((k_ref, k_s), (v_ref, v_s))):
            for side in range(2):
                at = pl.ds(side * half + step * width, width)
                sem = in_sems.at[step, 2 * i + side]
                loads.append(copy(src.at[:, at], dst.at[:, at], sem))
    for load in small + loads:
        load.start()
    for load in small:
        load.wait()
    t_s[:HD, :] = (q_s[...].astype(f32) * FACTOR).astype(bf16)
    t_s[HD:, :] = (d_s[...].astype(f32) * qm_s[...].astype(f32)).astype(bf16)
    stores = [copy(t_s, t_ref, out_sems.at[steps])]
    stores[0].start()
    mask = jnp.broadcast_to(m_s[...].astype(f32), (EXTRA, LANES)).astype(bf16)
    for step in range(steps):
        for load in loads[4 * step : 4 * step + 4]:
            load.wait()
        first = step * width // HD
        for j in range(first, first + width // HD, 2):
            for src, base in ((k_s, 0), (v_s, ROWS)):
                at = pl.ds(base, ROWS)
                low = src[:, j * HD : j * HD + LANES]
                high = src[:, half + j * HD : half + j * HD + LANES]
                kv_s[j, at, :] = jnp.concatenate([low[:, :HD], high[:, :HD]], axis=1)
                kv_s[j + 1, at, :] = jnp.concatenate([low[:, HD:], high[:, HD:]], axis=1)
            kv_s[j, 2 * ROWS :, :] = mask
            kv_s[j + 1, 2 * ROWS :, :] = mask
        at = pl.ds(first, width // HD)
        store = copy(kv_s.at[at], kv_ref.at[at], out_sems.at[step])
        store.start()
        stores.append(store)
    for store in stores:
        store.wait()


def unpack_kernel(g_ref, ko_ref, vo_ref, k_s, v_s, sems):
    steps = sems.shape[0]
    half = ko_ref.shape[1] // 2
    width = half // steps
    stores = []
    for step in range(steps):
        first = step * width // HD
        for i, (dst, out, base) in enumerate(((k_s, ko_ref, 0), (v_s, vo_ref, ROWS))):
            at = pl.ds(base, ROWS)
            for j in range(first, first + width // HD, 2):
                a = g_ref[j, at, :]
                b = g_ref[j + 1, at, :]
                low = jnp.concatenate([a[:, :HD], b[:, :HD]], axis=1)
                high = jnp.concatenate([a[:, HD:], b[:, HD:]], axis=1)
                dst[:, j * HD : j * HD + LANES] = low
                dst[:, half + j * HD : half + j * HD + LANES] = high
            for side in range(2):
                at = pl.ds(side * half + step * width, width)
                sem = sems.at[step, 2 * i + side]
                store = pltpu.make_async_copy(dst.at[:, at], out.at[:, at], sem)
                store.start()
                stores.append(store)
    for store in stores:
        store.wait()


def layer_index():
    return lax.axis_index("h") * 4 + lax.axis_index("s")


def spread_kernel(*refs):
    t_refs, (q_ref, d_ref, qt_ref, dt_ref, t_s) = refs[:LAYERS], refs[LAYERS:]
    layer = layer_index()
    for r in range(LAYERS):
        t_s[lax.rem(layer + LAYERS - r, LAYERS)] = t_refs[r][...]
    qt_ref[...] = jnp.zeros(qt_ref.shape, bf16)
    dt_ref[...] = jnp.zeros(dt_ref.shape, bf16)
    for block in range(TOKENS // ROWS):
        at = pl.ds(block * ROWS, ROWS)
        for head in range(2):
            mine = pl.ds(head * HD, HD)
            qt_ref[head, mine, at] = t_s[4 * head + block, :HD, :]
            dt_ref[head, mine, at] = t_s[4 * head + block, HD:, :]
            q_ref[head, at, :] = qt_ref[head, :, at].astype(f32).T.astype(bf16)
            d_ref[head, at, :] = dt_ref[head, :, at].astype(f32).T.astype(bf16)


def bias_of(k_ref, first):
    parts = []
    for i in range(JOINED):
        row = k_ref[first + i, 2 * ROWS :, :].astype(f32)
        square = column_of(row[:1, :])
        bias = jnp.where(square == 1.0, 0.0, MASKED_BIAS)
        parts.append(jnp.concatenate([bias] * (TOKENS // LANES), axis=1))
    return jnp.concatenate(parts, axis=0)


def block_of(k_ref, first, count, base):
    return k_ref[pl.ds(first, count), base : base + ROWS, :].reshape(count * ROWS, LANES)


SPLIT = (JOINED * ROWS // 8, 8, TOKENS)
FLAT = (JOINED * ROWS, TOKENS)


def stats_kernel(k_ref, qt_ref, dt_ref, o_ref, p_ref, b_ref, m_s, z_s, s_s):
    m_s[...] = jnp.full(m_s.shape, -3e38, f32)
    z_s[...] = jnp.zeros(z_s.shape, f32)
    s_s[...] = jnp.zeros(s_s.shape, f32)

    def one_step(step, carry):
        for part in range(UNROLLED):
            b = step * UNROLLED + part
            first = b * JOINED
            bias = bias_of(k_ref, first)
            keys = block_of(k_ref, first, JOINED, 0)
            values = block_of(k_ref, first, JOINED, ROWS)
            for head in range(2):
                logits = (dot(keys, qt_ref[head]) + bias).reshape(SPLIT)
                probs = dot(values, dt_ref[head]).reshape(SPLIT)
                old = m_s[head]
                new = jnp.maximum(old, jnp.max(logits, axis=0))
                scale = jnp.exp(old - new)
                weights = jnp.exp(logits - new[None])
                m_s[head] = new
                b_ref[head, b] = new
                z_s[head] = z_s[head] * scale + jnp.sum(weights, axis=0)
                s_s[head] = s_s[head] * scale + jnp.sum(weights * probs, axis=0)
                p_ref[head, b] = weights.reshape(FLAT).astype(bf16)
        return carry

    lax.fori_loop(0, PEERS // JOINED // UNROLLED, one_step, 0)
    for head in range(2):
        m = jnp.max(m_s[head], axis=0, keepdims=True)
        scale = jnp.exp(m_s[head] - m)
        z = jnp.sum(z_s[head] * scale, axis=0, keepdims=True)
        s = jnp.sum(s_s[head] * scale, axis=0, keepdims=True)
        for i, row in enumerate((m + jnp.log(z), s / z)):
            for half in range(2):
                at = 4 * i + 2 * head + half
                part = row[:, half * (TOKENS // 2) : (half + 1) * (TOKENS // 2)]
                for layer in range(LAYERS):
                    o_ref[layer, at : at + 1, :] = part


def grads_kernel(*refs):
    a_ref, k_ref, q_ref, d_ref, dt_ref, p_ref, b_ref, g_ref, gl_ref, kt_ref, sum_ref = refs[:11]
    l_s, r_s, gl_s, kt_s, g_s, sum_s, sems = refs[11:]
    for head in range(2):
        for half in range(2):
            at = 2 * head + half
            sums = [a_ref[i, at : at + 1, :] for i in range(LAYERS)]
            inner = [a_ref[i, 4 + at : 5 + at, :] for i in range(LAYERS)]
            m = functools.reduce(jnp.maximum, sums)
            shares = [jnp.exp(part - m) for part in sums]
            z = functools.reduce(jnp.add, shares)
            s = functools.reduce(jnp.add, [x * y for x, y in zip(shares, inner)])
            lanes = pl.ds(half * (TOKENS // 2), TOKENS // 2)
            l_s[head, :, lanes] = jnp.broadcast_to(m + jnp.log(z), (8, TOKENS // 2))
            r_s[head, :, lanes] = jnp.broadcast_to(s / z, (8, TOKENS // 2))

    count = MERGED * JOINED
    flat = (count * ROWS, TOKENS)
    parts = (MERGED,) + SPLIT

    steps = PEERS // count
    last = steps - 1

    def stores_of(step, is_last=False):
        at = pl.ds(step * count, count)
        if is_last:
            pairs = [(sum_s, sum_ref)]
        else:
            pairs = [(gl_s.at[head, step], gl_ref.at[head, step]) for head in range(2)]
            pairs += [(kt_s.at[step], kt_ref.at[step])]
        pairs += [(g_s.at[at], g_ref.at[at])]
        copy = pltpu.make_async_copy
        return [copy(src, dst, sems.at[step, i]) for i, (src, dst) in enumerate(pairs)]

    def one_step(step, is_last=False):
        first = step * count
        stores = stores_of(step, is_last)
        keys_t = block_of(k_ref, first, count, 0).astype(f32).T.astype(bf16)
        if not is_last:
            kt_s[step] = keys_t
            stores[2].start()
        values = block_of(k_ref, first, count, ROWS)
        both_weights, both_grads = [], []
        for head in range(2):
            blocks = pl.ds(MERGED * step, MERGED)
            scale = jnp.exp(b_ref[head, blocks] - l_s[head][None])
            probs = dot(values, dt_ref[head]).reshape(parts)
            weights = p_ref[head, blocks].astype(f32).reshape(parts) * scale[:, None]
            grad = weights * (probs - r_s[head])
            weights = weights.reshape(flat).astype(bf16)
            grad = grad.reshape(flat).astype(bf16)
            if is_last:
                sum_s[head] = dot(keys_t[head * HD : (head + 1) * HD, :], grad)
            else:
                gl_s[head, step] = grad
                stores[head].start()
            both_weights.append(weights)
            both_grads.append(grad)
        if is_last:
            stores[0].start()
        gv = dot(jnp.concatenate(both_weights, axis=1), d_ref[...].reshape(2 * TOKENS, LANES))
        gk = dot(jnp.concatenate(both_grads, axis=1), q_ref[...].reshape(2 * TOKENS, LANES))
        shape = (count, ROWS, LANES)
        g_s[pl.ds(first, count), :ROWS, :] = gk.astype(bf16).reshape(shape)
        g_s[pl.ds(first, count), ROWS:, :] = gv.astype(bf16).reshape(shape)
        stores[-1].start()

    def middle_step(step, carry):
        one_step(step)
        return carry

    lax.fori_loop(0, last, middle_step, 0)
    one_step(last, True)
    for step in range(steps):
        for store in stores_of(step, step == last):
            store.wait()


def query_kernel(gl_ref, kt_ref, sum_ref, *refs):
    gq_refs, (gl_s, kt_s, sum_s, part_s, sems, sum_sem) = refs[:LAYERS], refs[LAYERS:]
    steps = sems.shape[0]
    copy = pltpu.make_async_copy
    loads = []
    for step in range(steps):
        pairs = [(gl_ref.at[head, step], gl_s.at[head, step]) for head in range(2)]
        pairs += [(kt_ref.at[step], kt_s.at[step])]
        loads.append([copy(src, dst, sems.at[step, i]) for i, (src, dst) in enumerate(pairs)])
    rest = copy(sum_ref, sum_s, sum_sem)
    for load in [rest] + sum(loads, []):
        load.start()
    rest.wait()
    sums = [sum_s[0], sum_s[1]]
    for step in range(steps):
        for load in loads[step]:
            load.wait()
        for head in range(2):
            mine = kt_s[step, head * HD : (head + 1) * HD, :]
            sums[head] = sums[head] + dot(mine, gl_s[head, step])
    for block in range(TOKENS // ROWS):
        for head in range(2):
            part = sums[head][:, block * ROWS : (block + 1) * ROWS] * FACTOR
            part_s[4 * head + block] = part.astype(bf16)
    for r in range(LAYERS):
        gq_refs[r][...] = part_s[lax.rem(layer_index() + r, LAYERS)]


def permuted(array, distance):
    place = lambda z: (z % 4) * 2 + z // 4
    pairs = [(place(z), place((z + distance) % LAYERS)) for z in range(LAYERS)]
    return lax.ppermute(array, ("s", "h"), pairs)


def permuted_parts(arrays):
    return [arrays[0]] + [permuted(arrays[r], r) for r in range(1, LAYERS)]


def per_device(queries, keys, values, out_grad, key_mask, query_mask):
    vmem = pl.BlockSpec(memory_space=pltpu.VMEM)
    hbm = pl.BlockSpec(memory_space=pl.ANY)
    limit = lambda mib: pltpu.CompilerParams(vmem_limit_bytes=mib * MIB)
    whole = lambda *shape: pl.BlockSpec(shape, lambda i: (0,) * len(shape))
    scratch = lambda *shape, dtype=bf16: pltpu.VMEM(shape, dtype)
    dma = pltpu.SemaphoreType.DMA
    i32 = jnp.int32
    sent_rows = 2 * ROWS + EXTRA
    steps = 2
    packed, own_tokens = pl.pallas_call(
        pack_kernel,
        in_specs=[hbm] * 6,
        out_specs=[hbm] * 2,
        out_shape=[
            pltpu.HBM((PEERS, sent_rows, LANES), bf16),
            pltpu.HBM((2 * HD, ROWS), bf16),
        ],
        scratch_shapes=[
            scratch(*keys.shape),
            scratch(*values.shape),
            scratch(1, ROWS, dtype=i32),
            scratch(HD, ROWS),
            scratch(HD, ROWS),
            scratch(1, ROWS, dtype=i32),
            scratch(PEERS, sent_rows, LANES),
            scratch(2 * HD, ROWS),
            dma((steps, 4)),
            dma((4,)),
            dma((steps + 1,)),
        ],
        compiler_params=limit(60),
    )(
        keys,
        values,
        key_mask.reshape(1, ROWS),
        queries.T,
        out_grad.T,
        query_mask.reshape(1, ROWS),
    )
    exchange = functools.partial(lax.all_to_all, split_axis=0, concat_axis=0, tiled=True)
    rows = exchange(packed, PLANE)
    tokens = permuted_parts([own_tokens] * LAYERS)

    blocks = PEERS // JOINED
    shape = jax.ShapeDtypeStruct
    q, d, qt, dt = pl.pallas_call(
        spread_kernel,
        in_specs=[vmem] * LAYERS,
        out_specs=[vmem] * 4,
        out_shape=[shape((2, TOKENS, LANES), bf16)] * 2 + [shape((2, LANES, TOKENS), bf16)] * 2,
        scratch_shapes=[scratch(LAYERS, 2 * HD, ROWS)],
        compiler_params=limit(8),
    )(*tokens)
    stats, weights, maxima = pl.pallas_call(
        stats_kernel,
        in_specs=[vmem] * 3,
        out_specs=[vmem] * 3,
        out_shape=[
            shape((LAYERS, 8, TOKENS // 2), f32),
            shape((2, blocks) + FLAT, bf16),
            shape((2, blocks, 8, TOKENS), f32),
        ],
        scratch_shapes=[
            scratch(2, 8, TOKENS, dtype=f32),
            scratch(2, 8, TOKENS, dtype=f32),
            scratch(2, 8, TOKENS, dtype=f32),
        ],
        compiler_params=limit(24),
    )(rows, qt, dt)
    all_stats = exchange(stats, COLUMN)
    steps = blocks // MERGED
    merged = MERGED * JOINED * ROWS
    grads, grad_logits, keys_t, query_rest = pl.pallas_call(
        grads_kernel,
        in_specs=[vmem] * 7,
        out_specs=[hbm] * 4,
        out_shape=[
            pltpu.HBM((PEERS, 2 * ROWS, LANES), bf16),
            pltpu.HBM((2, steps - 1, merged, TOKENS), bf16),
            pltpu.HBM((steps - 1, LANES, merged), bf16),
            pltpu.HBM((2, HD, TOKENS), f32),
        ],
        scratch_shapes=[
            scratch(2, 8, TOKENS, dtype=f32),
            scratch(2, 8, TOKENS, dtype=f32),
            scratch(2, steps - 1, merged, TOKENS),
            scratch(steps - 1, LANES, merged),
            scratch(PEERS, 2 * ROWS, LANES),
            scratch(2, HD, TOKENS, dtype=f32),
            dma((steps, 4)),
        ],
        compiler_params=limit(38),
    )(all_stats, rows, q, d, dt, weights, maxima)
    own_rows = exchange(grads, PLANE)
    query_parts = pl.pallas_call(
        query_kernel,
        in_specs=[hbm] * 3,
        out_specs=[vmem] * LAYERS,
        out_shape=[shape((HD, ROWS), bf16)] * LAYERS,
        scratch_shapes=[
            scratch(2, steps - 1, merged, TOKENS),
            scratch(steps - 1, LANES, merged),
            scratch(2, HD, TOKENS, dtype=f32),
            scratch(LAYERS, HD, ROWS),
            dma((steps - 1, 3)),
            dma,
        ],
        compiler_params=limit(48),
        cost_estimate=pl.CostEstimate(
            flops=4 * PEERS * ROWS * HD * TOKENS, bytes_accessed=9 * MIB, transcendentals=0
        ),
    )(grad_logits, keys_t, query_rest)
    own_parts = permuted_parts(query_parts)
    total = functools.reduce(jnp.add, [part.astype(f32) for part in own_parts])
    grad_queries = total.astype(bf16).T
    grad_keys, grad_values = pl.pallas_call(
        unpack_kernel,
        in_specs=[vmem],
        out_specs=[hbm] * 2,
        out_shape=[pltpu.HBM(keys.shape, bf16), pltpu.HBM(values.shape, bf16)],
        scratch_shapes=[scratch(*keys.shape), scratch(*values.shape), dma((steps, 4))],
        compiler_params=limit(16),
    )(own_rows)
    return grad_queries, grad_keys, grad_values


def solution(mesh):
    fine = Mesh(mesh.devices.reshape(4, 2, 4, 4, 2), AXES)
    ctx = ("h",) + PLANE
    rows = ("s",) + ctx
    head_spec = P("s", ctx)
    row_spec = P(rows, None)
    return jax.shard_map(
        per_device,
        mesh=fine,
        in_specs=(head_spec, row_spec, row_spec, head_spec, P(rows), P("s")),
        out_specs=(head_spec, row_spec, row_spec),
        check_vma=False,
    )
```

```python
import functools
import math

import jax
import jax.numpy as jnp
from jax import lax
from jax.experimental import pallas as pl
from jax.experimental.pallas import tpu as pltpu
from jax.sharding import Mesh
from jax.sharding import PartitionSpec as P

HD = 64
LANES = 128
TOKENS = 512
ROWS = 128
EXTRA = 16
JOINED = 2
UNROLLED = 16
MERGED = 4
MIB = 1024 * 1024
FACTOR = 1.0 / math.sqrt(HD)
MASKED_BIAS = -1000000000.0
AXES = ("s", "h", "x", "y", "c")
PLANE = ("x", "y", "c")
COLUMN = ("h", "s")
PEERS = 32
LAYERS = 8
f32 = jnp.float32
bf16 = jnp.bfloat16
NT = (((1,), (1,)), ((), ()))
NN = (((1,), (0,)), ((), ()))


def dot(a, b, dims=NN):
    return lax.dot_general(a, b, dims, preferred_element_type=f32)


def column_of(row):
    return jnp.broadcast_to(row, (LANES, LANES)).T


def pack_kernel(k_ref, v_ref, m_ref, q_ref, d_ref, qm_ref, kv_ref, t_ref, *scratch):
    k_s, v_s, m_s, q_s, d_s, qm_s, kv_s, t_s, in_sems, small_sems, out_sems = scratch
    steps = in_sems.shape[0]
    half = k_ref.shape[1] // 2
    width = half // steps
    copy = pltpu.make_async_copy
    small = ((m_ref, m_s), (q_ref, q_s), (d_ref, d_s), (qm_ref, qm_s))
    small = [copy(src, dst, small_sems.at[i]) for i, (src, dst) in enumerate(small)]
    loads = []
    for step in range(steps):
        for i, (src, dst) in enumerate(((k_ref, k_s), (v_ref, v_s))):
            for side in range(2):
                at = pl.ds(side * half + step * width, width)
                sem = in_sems.at[step, 2 * i + side]
                loads.append(copy(src.at[:, at], dst.at[:, at], sem))
    for load in small + loads:
        load.start()
    for load in small:
        load.wait()
    t_s[:HD, :] = (q_s[...].astype(f32) * FACTOR).astype(bf16)
    t_s[HD:, :] = (d_s[...].astype(f32) * qm_s[...].astype(f32)).astype(bf16)
    stores = [copy(t_s, t_ref, out_sems.at[steps])]
    stores[0].start()
    mask = jnp.broadcast_to(m_s[...].astype(f32), (EXTRA, LANES)).astype(bf16)
    for step in range(steps):
        for load in loads[4 * step : 4 * step + 4]:
            load.wait()
        first = step * width // HD
        for j in range(first, first + width // HD, 2):
            for src, base in ((k_s, 0), (v_s, ROWS)):
                at = pl.ds(base, ROWS)
                low = src[:, j * HD : j * HD + LANES]
                high = src[:, half + j * HD : half + j * HD + LANES]
                kv_s[j, at, :] = jnp.concatenate([low[:, :HD], high[:, :HD]], axis=1)
                kv_s[j + 1, at, :] = jnp.concatenate([low[:, HD:], high[:, HD:]], axis=1)
            kv_s[j, 2 * ROWS :, :] = mask
            kv_s[j + 1, 2 * ROWS :, :] = mask
        at = pl.ds(first, width // HD)
        store = copy(kv_s.at[at], kv_ref.at[at], out_sems.at[step])
        store.start()
        stores.append(store)
    for store in stores:
        store.wait()


def unpack_kernel(g_ref, ko_ref, vo_ref, k_s, v_s, sems):
    steps = sems.shape[0]
    half = ko_ref.shape[1] // 2
    width = half // steps
    stores = []
    for step in range(steps):
        first = step * width // HD
        for i, (dst, out, base) in enumerate(((k_s, ko_ref, 0), (v_s, vo_ref, ROWS))):
            at = pl.ds(base, ROWS)
            for j in range(first, first + width // HD, 2):
                a = g_ref[j, at, :]
                b = g_ref[j + 1, at, :]
                low = jnp.concatenate([a[:, :HD], b[:, :HD]], axis=1)
                high = jnp.concatenate([a[:, HD:], b[:, HD:]], axis=1)
                dst[:, j * HD : j * HD + LANES] = low
                dst[:, half + j * HD : half + j * HD + LANES] = high
            for side in range(2):
                at = pl.ds(side * half + step * width, width)
                sem = sems.at[step, 2 * i + side]
                store = pltpu.make_async_copy(dst.at[:, at], out.at[:, at], sem)
                store.start()
                stores.append(store)
    for store in stores:
        store.wait()


def layer_index():
    return lax.axis_index("h") * 4 + lax.axis_index("s")


def spread_kernel(*refs):
    t_refs, (q_ref, d_ref, qt_ref, dt_ref, t_s) = refs[:LAYERS], refs[LAYERS:]
    layer = layer_index()
    for r in range(LAYERS):
        t_s[lax.rem(layer + LAYERS - r, LAYERS)] = t_refs[r][...]
    qt_ref[...] = jnp.zeros(qt_ref.shape, bf16)
    dt_ref[...] = jnp.zeros(dt_ref.shape, bf16)
    for block in range(TOKENS // ROWS):
        at = pl.ds(block * ROWS, ROWS)
        for head in range(2):
            mine = pl.ds(head * HD, HD)
            qt_ref[head, mine, at] = t_s[4 * head + block, :HD, :]
            dt_ref[head, mine, at] = t_s[4 * head + block, HD:, :]
            q_ref[head, at, :] = qt_ref[head, :, at].astype(f32).T.astype(bf16)
            d_ref[head, at, :] = dt_ref[head, :, at].astype(f32).T.astype(bf16)


def bias_of(k_ref, first):
    parts = []
    for i in range(JOINED):
        row = k_ref[first + i, 2 * ROWS :, :].astype(f32)
        square = column_of(row[:1, :])
        bias = jnp.where(square == 1.0, 0.0, MASKED_BIAS)
        parts.append(jnp.concatenate([bias] * (TOKENS // LANES), axis=1))
    return jnp.concatenate(parts, axis=0)


def block_of(k_ref, first, count, base):
    return k_ref[pl.ds(first, count), base : base + ROWS, :].reshape(count * ROWS, LANES)


SPLIT = (JOINED * ROWS // 8, 8, TOKENS)
FLAT = (JOINED * ROWS, TOKENS)


def stats_kernel(k_ref, qt_ref, dt_ref, o_ref, p_ref, b_ref, m_s, z_s, s_s):
    m_s[...] = jnp.full(m_s.shape, -3e38, f32)
    z_s[...] = jnp.zeros(z_s.shape, f32)
    s_s[...] = jnp.zeros(s_s.shape, f32)

    def one_step(step, carry):
        for part in range(UNROLLED):
            b = step * UNROLLED + part
            first = b * JOINED
            bias = bias_of(k_ref, first)
            keys = block_of(k_ref, first, JOINED, 0)
            values = block_of(k_ref, first, JOINED, ROWS)
            for head in range(2):
                logits = (dot(keys, qt_ref[head]) + bias).reshape(SPLIT)
                probs = dot(values, dt_ref[head]).reshape(SPLIT)
                old = m_s[head]
                new = jnp.maximum(old, jnp.max(logits, axis=0))
                scale = jnp.exp(old - new)
                weights = jnp.exp(logits - new[None])
                m_s[head] = new
                b_ref[head, b] = new
                z_s[head] = z_s[head] * scale + jnp.sum(weights, axis=0)
                s_s[head] = s_s[head] * scale + jnp.sum(weights * probs, axis=0)
                p_ref[head, b] = weights.reshape(FLAT).astype(bf16)
        return carry

    lax.fori_loop(0, PEERS // JOINED // UNROLLED, one_step, 0)
    for head in range(2):
        m = jnp.max(m_s[head], axis=0, keepdims=True)
        scale = jnp.exp(m_s[head] - m)
        z = jnp.sum(z_s[head] * scale, axis=0, keepdims=True)
        s = jnp.sum(s_s[head] * scale, axis=0, keepdims=True)
        for i, row in enumerate((m + jnp.log(z), s / z)):
            for half in range(2):
                at = 4 * i + 2 * head + half
                part = row[:, half * (TOKENS // 2) : (half + 1) * (TOKENS // 2)]
                for layer in range(LAYERS):
                    o_ref[layer, at : at + 1, :] = part


def grads_kernel(*refs):
    a_ref, k_ref, q_ref, d_ref, dt_ref, p_ref, b_ref, g_ref, gl_ref, kt_ref = refs[:10]
    l_s, r_s, gl_s, kt_s, g_s, sems = refs[10:]
    for head in range(2):
        for half in range(2):
            at = 2 * head + half
            sums = [a_ref[i, at : at + 1, :] for i in range(LAYERS)]
            inner = [a_ref[i, 4 + at : 5 + at, :] for i in range(LAYERS)]
            m = functools.reduce(jnp.maximum, sums)
            shares = [jnp.exp(part - m) for part in sums]
            z = functools.reduce(jnp.add, shares)
            s = functools.reduce(jnp.add, [x * y for x, y in zip(shares, inner)])
            lanes = pl.ds(half * (TOKENS // 2), TOKENS // 2)
            l_s[head, :, lanes] = jnp.broadcast_to(m + jnp.log(z), (8, TOKENS // 2))
            r_s[head, :, lanes] = jnp.broadcast_to(s / z, (8, TOKENS // 2))

    count = MERGED * JOINED
    flat = (count * ROWS, TOKENS)
    parts = (MERGED,) + SPLIT

    def stores_of(step):
        at = pl.ds(step * count, count)
        pairs = [(gl_s.at[head, step], gl_ref.at[head, step]) for head in range(2)]
        pairs += [(kt_s.at[step], kt_ref.at[step]), (g_s.at[at], g_ref.at[at])]
        copy = pltpu.make_async_copy
        return [copy(src, dst, sems.at[step, i]) for i, (src, dst) in enumerate(pairs)]

    def one_step(step, carry):
        first = step * count
        stores = stores_of(step)
        kt_s[step] = block_of(k_ref, first, count, 0).astype(f32).T.astype(bf16)
        stores[2].start()
        values = block_of(k_ref, first, count, ROWS)
        both_weights, both_grads = [], []
        for head in range(2):
            blocks = pl.ds(MERGED * step, MERGED)
            scale = jnp.exp(b_ref[head, blocks] - l_s[head][None])
            probs = dot(values, dt_ref[head]).reshape(parts)
            weights = p_ref[head, blocks].astype(f32).reshape(parts) * scale[:, None]
            grad = weights * (probs - r_s[head])
            weights = weights.reshape(flat).astype(bf16)
            grad = grad.reshape(flat).astype(bf16)
            gl_s[head, step] = grad
            stores[head].start()
            both_weights.append(weights)
            both_grads.append(grad)
        gv = dot(jnp.concatenate(both_weights, axis=1), d_ref[...].reshape(2 * TOKENS, LANES))
        gk = dot(jnp.concatenate(both_grads, axis=1), q_ref[...].reshape(2 * TOKENS, LANES))
        shape = (count, ROWS, LANES)
        g_s[pl.ds(first, count), :ROWS, :] = gk.astype(bf16).reshape(shape)
        g_s[pl.ds(first, count), ROWS:, :] = gv.astype(bf16).reshape(shape)
        stores[3].start()
        return carry

    steps = PEERS // count
    lax.fori_loop(0, steps, one_step, 0)
    for step in range(steps):
        for store in stores_of(step):
            store.wait()


def query_kernel(gl_ref, kt_ref, *refs):
    gq_refs, (gl_s, kt_s, part_s, sems) = refs[:LAYERS], refs[LAYERS:]
    steps = sems.shape[0]
    copy = pltpu.make_async_copy
    loads = []
    for step in range(steps):
        pairs = [(gl_ref.at[head, step], gl_s.at[head, step]) for head in range(2)]
        pairs += [(kt_ref.at[step], kt_s.at[step])]
        loads.append([copy(src, dst, sems.at[step, i]) for i, (src, dst) in enumerate(pairs)])
    for load in sum(loads, []):
        load.start()
    sums = [0.0, 0.0]
    for step in range(steps):
        for load in loads[step]:
            load.wait()
        for head in range(2):
            mine = kt_s[step, head * HD : (head + 1) * HD, :]
            sums[head] = sums[head] + dot(mine, gl_s[head, step])
    for block in range(TOKENS // ROWS):
        for head in range(2):
            part = sums[head][:, block * ROWS : (block + 1) * ROWS] * FACTOR
            part_s[4 * head + block] = part.astype(bf16)
    for r in range(LAYERS):
        gq_refs[r][...] = part_s[lax.rem(layer_index() + r, LAYERS)]


def permuted(array, distance):
    place = lambda z: (z % 4) * 2 + z // 4
    pairs = [(place(z), place((z + distance) % LAYERS)) for z in range(LAYERS)]
    return lax.ppermute(array, ("s", "h"), pairs)


def permuted_parts(arrays):
    return [arrays[0]] + [permuted(arrays[r], r) for r in range(1, LAYERS)]


def per_device(queries, keys, values, out_grad, key_mask, query_mask):
    vmem = pl.BlockSpec(memory_space=pltpu.VMEM)
    hbm = pl.BlockSpec(memory_space=pl.ANY)
    limit = lambda mib: pltpu.CompilerParams(vmem_limit_bytes=mib * MIB)
    whole = lambda *shape: pl.BlockSpec(shape, lambda i: (0,) * len(shape))
    scratch = lambda *shape, dtype=bf16: pltpu.VMEM(shape, dtype)
    dma = pltpu.SemaphoreType.DMA
    i32 = jnp.int32
    sent_rows = 2 * ROWS + EXTRA
    steps = 2
    packed, own_tokens = pl.pallas_call(
        pack_kernel,
        in_specs=[hbm] * 6,
        out_specs=[hbm] * 2,
        out_shape=[
            pltpu.HBM((PEERS, sent_rows, LANES), bf16),
            pltpu.HBM((2 * HD, ROWS), bf16),
        ],
        scratch_shapes=[
            scratch(*keys.shape),
            scratch(*values.shape),
            scratch(1, ROWS, dtype=i32),
            scratch(HD, ROWS),
            scratch(HD, ROWS),
            scratch(1, ROWS, dtype=i32),
            scratch(PEERS, sent_rows, LANES),
            scratch(2 * HD, ROWS),
            dma((steps, 4)),
            dma((4,)),
            dma((steps + 1,)),
        ],
        compiler_params=limit(60),
    )(
        keys,
        values,
        key_mask.reshape(1, ROWS),
        queries.T,
        out_grad.T,
        query_mask.reshape(1, ROWS),
    )
    exchange = functools.partial(lax.all_to_all, split_axis=0, concat_axis=0, tiled=True)
    rows = exchange(packed, PLANE)
    tokens = permuted_parts([own_tokens] * LAYERS)

    blocks = PEERS // JOINED
    shape = jax.ShapeDtypeStruct
    q, d, qt, dt = pl.pallas_call(
        spread_kernel,
        in_specs=[vmem] * LAYERS,
        out_specs=[vmem] * 4,
        out_shape=[shape((2, TOKENS, LANES), bf16)] * 2 + [shape((2, LANES, TOKENS), bf16)] * 2,
        scratch_shapes=[scratch(LAYERS, 2 * HD, ROWS)],
        compiler_params=limit(8),
    )(*tokens)
    stats, weights, maxima = pl.pallas_call(
        stats_kernel,
        in_specs=[vmem] * 3,
        out_specs=[vmem] * 3,
        out_shape=[
            shape((LAYERS, 8, TOKENS // 2), f32),
            shape((2, blocks) + FLAT, bf16),
            shape((2, blocks, 8, TOKENS), f32),
        ],
        scratch_shapes=[
            scratch(2, 8, TOKENS, dtype=f32),
            scratch(2, 8, TOKENS, dtype=f32),
            scratch(2, 8, TOKENS, dtype=f32),
        ],
        compiler_params=limit(24),
    )(rows, qt, dt)
    all_stats = exchange(stats, COLUMN)
    steps = blocks // MERGED
    merged = MERGED * JOINED * ROWS
    grads, grad_logits, keys_t = pl.pallas_call(
        grads_kernel,
        in_specs=[vmem] * 7,
        out_specs=[hbm] * 3,
        out_shape=[
            pltpu.HBM((PEERS, 2 * ROWS, LANES), bf16),
            pltpu.HBM((2, steps, merged, TOKENS), bf16),
            pltpu.HBM((steps, LANES, merged), bf16),
        ],
        scratch_shapes=[
            scratch(2, 8, TOKENS, dtype=f32),
            scratch(2, 8, TOKENS, dtype=f32),
            scratch(2, steps, merged, TOKENS),
            scratch(steps, LANES, merged),
            scratch(PEERS, 2 * ROWS, LANES),
            dma((steps, 4)),
        ],
        compiler_params=limit(38),
    )(all_stats, rows, q, d, dt, weights, maxima)
    own_rows = exchange(grads, PLANE)
    query_parts = pl.pallas_call(
        query_kernel,
        in_specs=[hbm] * 2,
        out_specs=[vmem] * LAYERS,
        out_shape=[shape((HD, ROWS), bf16)] * LAYERS,
        scratch_shapes=[
            scratch(2, steps, merged, TOKENS),
            scratch(steps, LANES, merged),
            scratch(LAYERS, HD, ROWS),
            dma((steps, 3)),
        ],
        compiler_params=limit(48),
        cost_estimate=pl.CostEstimate(
            flops=4 * PEERS * ROWS * HD * TOKENS, bytes_accessed=9 * MIB, transcendentals=0
        ),
    )(grad_logits, keys_t)
    own_parts = permuted_parts(query_parts)
    total = functools.reduce(jnp.add, [part.astype(f32) for part in own_parts])
    grad_queries = total.astype(bf16).T
    grad_keys, grad_values = pl.pallas_call(
        unpack_kernel,
        in_specs=[vmem],
        out_specs=[hbm] * 2,
        out_shape=[pltpu.HBM(keys.shape, bf16), pltpu.HBM(values.shape, bf16)],
        scratch_shapes=[scratch(*keys.shape), scratch(*values.shape), dma((steps, 4))],
        compiler_params=limit(16),
    )(own_rows)
    return grad_queries, grad_keys, grad_values


def solution(mesh):
    fine = Mesh(mesh.devices.reshape(4, 2, 4, 4, 2), AXES)
    ctx = ("h",) + PLANE
    rows = ("s",) + ctx
    head_spec = P("s", ctx)
    row_spec = P(rows, None)
    return jax.shard_map(
        per_device,
        mesh=fine,
        in_specs=(head_spec, row_spec, row_spec, head_spec, P(rows), P("s")),
        out_specs=(head_spec, row_spec, row_spec),
        check_vma=False,
    )
```
